32 devices in a mesh: fsdp: 16 (over z, y, x), tp: 2 (over core).
Axes of the slice: x: 2, y: 2, z: 4, core: 2. Of those that a mesh axis runs over, the one named last changes fastest.
Arguments:
- tokens_in: bfloat16 [4096, 2560], P(('fsdp', 'tp')), may hold values from -6 to 6
- cotangent: bfloat16 [4096, 2560], P(('fsdp', 'tp')), may hold values from -6 to 6
- doc_ids: int32 [4096], P('fsdp'), may hold values from 0 to 2, as said below
- routes: int32 [4096, 6], P('fsdp'), may hold values from 0 to 15, all different within a row; in each aligned block of 256 rows (0 to 255, 256 to 511, ...) at most 128 rows name the same one
- gain_attn: bfloat16 [2560], P('fsdp'), may hold values from 0.5 to 1.5
- w_query: bfloat16 [2560, 2560], P('fsdp', 'tp'), may hold values from -0.125 to 0.125
- w_key: bfloat16 [2560, 512], P('fsdp', 'tp'), may hold values from -0.125 to 0.125
- w_value: bfloat16 [2560, 512], P('fsdp', 'tp'), may hold values from -0.125 to 0.125
- w_out: bfloat16 [2560, 2560], P('tp', 'fsdp'), may hold values from -0.625 to 0.625
- gain_ffn: bfloat16 [2560], P('fsdp'), may hold values from 0.5 to 1.5
- w_router: bfloat16 [2560, 16], P('fsdp'), may hold values from -0.0625 to 0.0625
- w_shared_gate: bfloat16 [2560, 3072], P('fsdp', 'tp'), may hold values from -0.125 to 0.125
- w_shared_up: bfloat16 [2560, 3072], P('fsdp', 'tp'), may hold values from -0.125 to 0.125
- w_shared_down: bfloat16 [3072, 2560], P('tp', 'fsdp'), may hold values from -0.109375 to 0.109375
- w_expert_gate: bfloat16 [16, 2560, 1536], P('fsdp', None, 'tp'), may hold values from -0.125 to 0.125
- w_expert_up: bfloat16 [16, 2560, 1536], P('fsdp', None, 'tp'), may hold values from -0.125 to 0.125
- w_expert_down: bfloat16 [16, 1536, 2560], P('fsdp', 'tp'), may hold values from -0.3125 to 0.3125
Outputs:
- block_out: bfloat16 [4096, 2560], P(('fsdp', 'tp'))
- grad_tokens: float32 [4096, 2560], P(('fsdp', 'tp'))
- grad_gain_attn: float32 [2560], P('fsdp')
- grad_query: float32 [2560, 2560], P('fsdp', 'tp')
- grad_key: float32 [2560, 512], P('fsdp', 'tp')
- grad_value: float32 [2560, 512], P('fsdp', 'tp')
- grad_out: float32 [2560, 2560], P('tp', 'fsdp')
- grad_gain_ffn: float32 [2560], P('fsdp')
- grad_router: float32 [2560, 16], P('fsdp')
- grad_shared_gate: float32 [2560, 3072], P('fsdp', 'tp')
- grad_shared_up: float32 [2560, 3072], P('fsdp', 'tp')
- grad_shared_down: float32 [3072, 2560], P('tp', 'fsdp')
- grad_expert_gate: float32 [16, 2560, 1536], P('fsdp', None, 'tp')
- grad_expert_up: float32 [16, 2560, 1536], P('fsdp', None, 'tp')
- grad_expert_down: float32 [16, 1536, 2560], P('fsdp', 'tp')
The draws below stay inside these ranges and needn't reach their ends.
Inputs may be any that keep to these rules, and one draw needn't show every extreme that they name: `doc_ids`: each sequence's tokens are numbered 0, 1, 2 by document, never falling; every number occurs. `routes`: among the 256 tokens of one sequence no expert is named more than 128 times, a bound that some block reaches.
All inputs are finite; a program needn't handle non-finite values.
Results may differ from the reference program's by a relative error of at most 0.017.
Values may be sent and summed in bfloat16 or wider, within the bound.
No kernel may reach another device: no remote copies, remote signals or barrier semaphores. Data moves between devices by JAX's collectives and lax.ppermute only.
A program may use at most 320 MiB of HBM per device.

```python
import math
import jax
import jax.numpy as jnp
import numpy as np
from jax import lax

D = 2560
QUERY_HEADS = 20
KEY_VALUE_HEADS = 4
HEAD_SIZE = 128
FE = 1536
TOPK = 6
SEQ_LEN = 256
SH = 3072
QD = 2560
KVD = 512
EXPERTS = 16
CAP = 128
TOKENS = 4096
N_FSDP = 16
N_TP = 2


def draw_doc_ids(key, part):
    key = jax.random.fold_in(key, 7)
    groups = TOKENS // SEQ_LEN
    first_key, second_key = jax.random.split(key)
    first_cut = jax.random.randint(first_key, (groups, 1), SEQ_LEN // 8, 3 * SEQ_LEN // 8)
    second_cut = jax.random.randint(second_key, (groups, 1), 5 * SEQ_LEN // 8, 7 * SEQ_LEN // 8)
    places = jnp.arange(SEQ_LEN, dtype=jnp.int32)[None, :]
    numbers = (places >= first_cut).astype(jnp.int32) + (places >= second_cut).astype(jnp.int32)
    return numbers.reshape(TOKENS)


def block_scale(rng, extent, pieces, smallest, top_value):
    loudness, own = 1.0, jax.random.fold_in(rng, 6)
    for axis_at, parts in pieces:
        heights = jnp.exp(jax.random.uniform(jax.random.fold_in(own, axis_at), (parts,), jnp.float32, smallest / len(pieces), top_value / len(pieces)))
        loudness = loudness * jnp.repeat(heights, extent[axis_at] // parts).reshape([-1 if axis == axis_at else 1 for axis in range(len(extent))])
    return loudness


def routed_block(key, own, number, rows, count, top, reach, skew):
    ranking = jax.random.permutation(key, count)
    packed, ordinary = load_shares(count, rows * top, reach, skew, True), load_shares(count, rows * top, reach, skew, False)
    places = jnp.arange(count)

    def named(lengths, rotation):
        used = int((lengths > 0).sum())
        fixed = max(1, used // 4)
        passed = fixed + (places - fixed + rotation * (used - fixed)) % max(1, count - fixed)
        return jnp.zeros((count,), jnp.int32).at[ranking[jnp.where(places < fixed, places, passed)]].set(jnp.asarray(lengths, jnp.int32))

    lengths = jnp.where(number % 4 == 0, named(packed, number // 4), named(ordinary, number - number // 4 - 1))
    mixed = jax.random.permutation(jax.random.fold_in(own, 3), count)
    source_of, sink = mixed[0:count // 2 * 2:2], mixed[1:count // 2 * 2:2]
    margin = jnp.minimum(lengths[source_of] - 1, reach - lengths[sink]) // 2
    margin = jnp.where((source_of == ranking[0]) | (sink == ranking[0]) | (lengths[sink] == 0), 0, jnp.maximum(margin, 0))
    passed = jax.random.randint(jax.random.fold_in(own, 4), (count // 2,), 0, 1 << 20) % (margin + 1)
    lengths = lengths.at[source_of].add(-passed).at[sink].add(passed)
    items = jnp.searchsorted(jnp.cumsum(lengths), jnp.arange(rows * top), side="right").astype(jnp.int32)
    grid = items.reshape(top, rows).T
    grid = grid[jax.random.permutation(jax.random.fold_in(own, 1), rows)]
    rotation = jax.random.randint(jax.random.fold_in(own, 2), (rows, 1), 0, top)
    return jnp.take_along_axis(grid, (jnp.arange(top)[None, :] + rotation) % top, axis=1)


def load_shares(amount, total, limit, lean, full):
    portions = [(1 << 20) // math.isqrt(rank ** lean) + 1 for rank in range(1, amount + 1)]
    largest = limit if full else min(limit, max(-(-total // amount), total * portions[0] // sum(portions)))
    least = 1 if total - largest >= amount - 1 else 0
    given, surplus = [largest] + [least] * (amount - 1), total - largest - least * (amount - 1)
    while surplus > 0:
        free = [i for i in range(1, amount) if given[i] < largest] or [i for i in range(1, amount) if given[i] < limit]
        mass, budget = sum([portions[i] for i in free]), surplus
        for i in free:
            extra = min(limit - given[i], max(1, budget * portions[i] // mass), surplus)
            given[i] = given[i] + extra
            surplus = surplus - extra
    return np.array(given)


def normal_values(key, dims, scale, reach, shards=(), held_as=jnp.bfloat16):
    factor_of = block_scale(key, dims, shards, -0.22, 0.18) if shards else 1.0
    values = jax.random.normal(key, dims, jnp.float32) * scale * factor_of
    return jnp.minimum(jnp.maximum(values, -reach), reach).astype(held_as)


def setup_inputs(seed: int = 0) -> dict:
    keys = jax.random.split(jax.random.key(seed), 18)
    tokens_in = normal_values(keys[0], (TOKENS, D), 1.0, 6.0, ((0, 32),))
    cotangent = normal_values(keys[1], (TOKENS, D), 1.0, 6.0, ((0, 32),))
    doc_ids = draw_doc_ids(jax.random.fold_in(keys[17], 71), 0)
    routes_keys = jax.random.split(jax.random.fold_in(keys[3], 1), TOKENS // SEQ_LEN)
    routes_turns = jax.random.permutation(jax.random.fold_in(keys[3], 3), TOKENS // SEQ_LEN)
    routes = jax.vmap(lambda own, number: routed_block(jax.random.fold_in(keys[3], 2), own, number, SEQ_LEN, EXPERTS, TOPK, CAP, 1))(routes_keys, routes_turns).reshape((TOKENS, TOPK))
    gain_attn = jnp.clip(1.0 + 0.1 * jax.random.normal(keys[4], (D,), jnp.float32), 0.5, 1.5).astype(jnp.bfloat16)
    w_query = normal_values(keys[5], (D, QD), D ** -0.5, 0.125, ((0, 16), (1, 2)))
    w_key = normal_values(keys[6], (D, KVD), D ** -0.5, 0.125, ((0, 16), (1, 2)))
    w_value = normal_values(keys[7], (D, KVD), D ** -0.5, 0.125, ((0, 16), (1, 2)))
    w_out = normal_values(keys[8], (QD, D), (QD // 32) ** -0.5, 0.625, ((0, 2), (1, 16)))
    gain_ffn = jnp.clip(1.0 + 0.1 * jax.random.normal(keys[9], (D,), jnp.float32), 0.5, 1.5).astype(jnp.bfloat16)
    w_router = normal_values(keys[10], (D, EXPERTS), (4 * D) ** -0.5, 0.0625, ((0, 16),))
    w_shared_gate = normal_values(keys[11], (D, SH), D ** -0.5, 0.125, ((0, 16), (1, 2)))
    w_shared_up = normal_values(keys[12], (D, SH), D ** -0.5, 0.125, ((0, 16), (1, 2)))
    w_shared_down = normal_values(keys[13], (SH, D), SH ** -0.5, 0.109375, ((0, 2), (1, 16)))
    w_expert_gate = normal_values(keys[14], (EXPERTS, D, FE), D ** -0.5, 0.125, ((0, 16), (2, 2)))
    w_expert_up = normal_values(keys[15], (EXPERTS, D, FE), D ** -0.5, 0.125, ((0, 16), (2, 2)))
    w_expert_down = normal_values(keys[16], (EXPERTS, FE, D), (FE // 4) ** -0.5, 0.3125, ((0, 16), (1, 2)))
    return dict(tokens_in=tokens_in, cotangent=cotangent, doc_ids=doc_ids, routes=routes, gain_attn=gain_attn, w_query=w_query, w_key=w_key, w_value=w_value, w_out=w_out, gain_ffn=gain_ffn, w_router=w_router, w_shared_gate=w_shared_gate, w_shared_up=w_shared_up, w_shared_down=w_shared_down, w_expert_gate=w_expert_gate, w_expert_up=w_expert_up, w_expert_down=w_expert_down)


@jax.custom_vjp
def to_bfloat(v):
    return lax.optimization_barrier(v.astype(jnp.bfloat16)).astype(jnp.float32)

@jax.custom_vjp
def bfloat_backward(v):
    return v

def low_keep(v):
    return (to_bfloat(v), None)

def low_pass(kept, grad):
    return (grad,)

def back_keep(v):
    return (v, None)

def back_low(kept, grad):
    return (to_bfloat(grad),)
to_bfloat.defvjp(low_keep, low_pass)
bfloat_backward.defvjp(back_keep, back_low)
norm_eps = 1e-05
rope_base = 500000.0
highest = lax.Precision.HIGHEST

def matrix_product(left_mat, right_mat):
    return jnp.dot(left_mat, right_mat, precision=highest, preferred_element_type=jnp.float32)

def rms_norm(values, gain_vec):
    inv_rms = lax.rsqrt(lax.optimization_barrier(jnp.mean(values * values, axis=-1, keepdims=True)) + norm_eps)
    return values * inv_rms * gain_vec

def smooth_gate(values):
    return values / (1.0 + jnp.exp(-values))

def rotary_tables(length_total):
    half_width = HEAD_SIZE // 2
    inverse = 1.0 / rope_base ** (jnp.arange(half_width, dtype=jnp.float32) * (2.0 / HEAD_SIZE))
    angles = jnp.arange(length_total, dtype=jnp.float32)[:, None] * inverse[None, :]
    return (jnp.cos(angles), jnp.sin(angles))

def apply_rotary(values, rotary_cosine, rotary_sine):
    half_width = values.shape[-1] // 2
    first_half = values[..., :half_width]
    second_half = values[..., half_width:]
    cos_rows = rotary_cosine[:, None, :]
    sin_rows = rotary_sine[:, None, :]
    return jnp.concatenate([first_half * cos_rows - second_half * sin_rows, second_half * cos_rows + first_half * sin_rows], axis=-1)

def attend(row_block_size, id_block, query_weight, key_weight, value_weight, rotary_cosine, rotary_sine):
    length_total = row_block_size.shape[0]
    tokens_per_group = QUERY_HEADS // KEY_VALUE_HEADS
    query_states = to_bfloat(apply_rotary(bfloat_backward(matrix_product(row_block_size, query_weight)).reshape(length_total, QUERY_HEADS, HEAD_SIZE), rotary_cosine, rotary_sine))
    query_states = query_states.reshape(length_total, KEY_VALUE_HEADS, tokens_per_group, HEAD_SIZE)
    rotated_key = to_bfloat(apply_rotary(bfloat_backward(matrix_product(row_block_size, key_weight)).reshape(length_total, KEY_VALUE_HEADS, HEAD_SIZE), rotary_cosine, rotary_sine))
    value_states = to_bfloat(bfloat_backward(matrix_product(row_block_size, value_weight))).reshape(length_total, KEY_VALUE_HEADS, HEAD_SIZE)
    scores = bfloat_backward(jnp.einsum('qgjd,kgd->gjqk', query_states, rotated_key, precision=highest) * HEAD_SIZE ** (-0.5))
    order_ids = jnp.arange(length_total)
    allowed = (id_block[:, None] == id_block[None, :]) & (order_ids[:, None] >= order_ids[None, :])
    scores = jnp.where(allowed, scores, -1e+30)
    top_score = lax.optimization_barrier(jnp.max(scores, axis=-1, keepdims=True))
    weights = jnp.exp(scores - top_score)
    attn_probs = to_bfloat(weights / lax.optimization_barrier(jnp.sum(weights, axis=-1, keepdims=True)))
    mixed = jnp.einsum('gjqk,kgd->qgjd', attn_probs, value_states, precision=highest)
    return to_bfloat(bfloat_backward(mixed.reshape(length_total, QUERY_HEADS * HEAD_SIZE)))

def reference(tokens_in, cotangent, doc_ids, routes, gain_attn, w_query, w_key, w_value, w_out, gain_ffn, w_router, w_shared_gate, w_shared_up, w_shared_down, w_expert_gate, w_expert_up, w_expert_down):
    total_rows = tokens_in.shape[0]
    groups = total_rows // SEQ_LEN
    flat_routes = routes.reshape(-1).astype(jnp.int32)
    slots_most = N_FSDP * CAP
    sort_order = jnp.argsort(flat_routes, stable=True).astype(jnp.int32)
    counts = lax.optimization_barrier(jnp.sum((flat_routes[None, :] == jnp.arange(EXPERTS, dtype=jnp.int32)[:, None]).astype(jnp.int32), axis=1)).astype(jnp.int32)
    starts = (jnp.cumsum(counts) - counts).astype(jnp.int32)
    offsets = jnp.arange(slots_most, dtype=jnp.int32)
    selected_rows = sort_order[jnp.minimum(starts[:, None] + offsets[None, :], flat_routes.shape[0] - 1)]
    valid_row_mask = (offsets[None, :] < counts[:, None]).astype(jnp.float32)
    block_width = FE // N_TP

    def layer_forward(token_states, first_norm_gain, query_weight, key_weight, value_weight, output_weight, second_norm_gain, router_weight, shared_gate_weight, shared_up_weight, shared_down_weight, expert_gate_weight, expert_up_weight, expert_down_weight):
        normed_low = to_bfloat(rms_norm(token_states, first_norm_gain))
        rotary_cosine, rotary_sine = rotary_tables(SEQ_LEN)

        def one_sequence(item_pair):
            row_block_size, id_block = item_pair
            return attend(row_block_size, id_block, query_weight, key_weight, value_weight, rotary_cosine, rotary_sine)
        heads = lax.map(jax.checkpoint(one_sequence), (normed_low.reshape(groups, SEQ_LEN, D), doc_ids.reshape(groups, SEQ_LEN)))
        attn_branch = bfloat_backward(matrix_product(heads.reshape(total_rows, QD), output_weight))
        middle = token_states + attn_branch
        ffn_in = to_bfloat(rms_norm(middle, second_norm_gain))
        logits = bfloat_backward(matrix_product(ffn_in, router_weight))
        chosen = routes[:, :, None] == jnp.arange(EXPERTS, dtype=jnp.int32)[None, None, :]
        picked = lax.optimization_barrier(jnp.sum(jnp.where(chosen, logits[:, None, :], 0.0), axis=-1))
        top_pick = lax.optimization_barrier(jnp.max(picked, axis=-1, keepdims=True))
        gate_exp = jnp.exp(picked - top_pick)
        gate_values = gate_exp / lax.optimization_barrier(jnp.sum(gate_exp, axis=-1, keepdims=True))
        shared_gate = bfloat_backward(matrix_product(ffn_in, shared_gate_weight))
        shared_up = bfloat_backward(matrix_product(ffn_in, shared_up_weight))
        shared_hidden = to_bfloat(smooth_gate(shared_gate) * shared_up)
        shared_out = matrix_product(shared_hidden, shared_down_weight)
        flat_gates = gate_values.reshape(-1)

        def single_expert(item_pair):
            gate_mat, up_mat, down_mat, picks_here, valid_here = item_pair
            inputs = ffn_in[picks_here // TOPK]
            summed = jnp.zeros((slots_most, D), jnp.float32)
            for block_index in range(N_TP):
                start_col = block_index * block_width
                stop_col = start_col + block_width
                entry_rows = bfloat_backward(inputs)
                gate_part = bfloat_backward(matrix_product(entry_rows, gate_mat[:, start_col:stop_col]))
                up_part = bfloat_backward(matrix_product(entry_rows, up_mat[:, start_col:stop_col]))
                hidden = to_bfloat(smooth_gate(gate_part) * up_part)
                summed = summed + to_bfloat(matrix_product(hidden, down_mat[start_col:stop_col, :]))
            return bfloat_backward(summed) * (flat_gates[picks_here] * valid_here)[:, None]
        rows_per_expert = lax.map(jax.checkpoint(single_expert), (expert_gate_weight, expert_up_weight, expert_down_weight, selected_rows, valid_row_mask))
        routed = jnp.zeros((total_rows, D), jnp.float32).at[(selected_rows // TOPK).reshape(-1)].add(rows_per_expert.reshape(-1, D))
        return middle + shared_out + routed
    primals = tuple((operand.astype(jnp.float32) for operand in (tokens_in, gain_attn, w_query, w_key, w_value, w_out, gain_ffn, w_router, w_shared_gate, w_shared_up, w_shared_down, w_expert_gate, w_expert_up, w_expert_down)))
    output, pullback = jax.vjp(layer_forward, *primals)
    gradients = pullback(cotangent.astype(jnp.float32))
    return (output.astype(jnp.bfloat16), gradients[0], gradients[1], gradients[2], gradients[3], gradients[4], gradients[5], gradients[6], gradients[7], gradients[8], gradients[9], gradients[10], gradients[11], gradients[12], gradients[13])
```

```python
import jax
import jax.numpy as jnp
from jax import lax
from jax.experimental import pallas as pl
from jax.experimental.pallas import tpu as pltpu
from jax.sharding import PartitionSpec as P

QUERY_HEADS = 20
KEY_VALUE_HEADS = 4
HEAD_SIZE = 128
TOPK = 6


norm_eps = 1e-05
rope_base = 500000.0


def rotary_tables(length_total):
    half_width = HEAD_SIZE // 2
    inverse = 1.0 / rope_base ** (jnp.arange(half_width, dtype=jnp.float32) * (2.0 / HEAD_SIZE))
    angles = jnp.arange(length_total, dtype=jnp.float32)[:, None] * inverse[None, :]
    return (jnp.cos(angles), jnp.sin(angles))


def apply_rotary(values, rotary_cosine, rotary_sine):
    half_width = values.shape[-1] // 2
    first_half = values[..., :half_width]
    second_half = values[..., half_width:]
    cos_rows = rotary_cosine[:, None, :]
    sin_rows = rotary_sine[:, None, :]
    return jnp.concatenate(
        [
            first_half * cos_rows - second_half * sin_rows,
            second_half * cos_rows + first_half * sin_rows,
        ],
        axis=-1,
    )


def smooth_gate(values):
    return values / (1.0 + jnp.exp(-values))


def smooth_slope(values):
    sigmoid = 1.0 / (1.0 + jnp.exp(-values))
    return sigmoid * (1.0 + values * (1.0 - sigmoid))


def rms_scale(values):
    return lax.rsqrt(jnp.mean(values * values, axis=-1, keepdims=True) + norm_eps)


def norm_back(grad_in, normed, inv_rms, gain_vec):
    scaled = grad_in * gain_vec
    return inv_rms * (scaled - normed * jnp.mean(scaled * normed, axis=-1, keepdims=True))


def product(left_mat, right_mat):
    return jnp.dot(left_mat, right_mat, preferred_element_type=jnp.float32)


def times_transposed(left_mat, right_mat):
    return lax.dot_general(
        left_mat, right_mat, (((1,), (1,)), ((), ())), preferred_element_type=jnp.float32
    )


def transposed_times(left_mat, right_mat):
    return lax.dot_general(
        left_mat, right_mat, (((0,), (0,)), ((), ())), preferred_element_type=jnp.float32
    )


def attention_scores(query_rot, rotated_key, allowed):
    scores = jnp.einsum(
        "qgjd,kgd->gjqk", query_rot, rotated_key, preferred_element_type=jnp.float32
    ) * HEAD_SIZE ** (-0.5)
    return jnp.where(allowed, scores, -1e30)


def shards(
    tokens_in,
    cotangent,
    doc_ids,
    routes,
    gain_attn,
    w_query,
    w_key,
    w_value,
    w_out,
    gain_ffn,
    w_router,
    w_shared_gate,
    w_shared_up,
    w_shared_down,
    w_expert_gate,
    w_expert_up,
    w_expert_down,
):
    own_rows = tokens_in.shape[0]
    seq_rows = doc_ids.shape[0]
    model_width = tokens_in.shape[1]
    experts = w_router.shape[1]
    local_experts = w_expert_gate.shape[0]
    sources = experts // local_experts
    capacity = max(2, 4 * seq_rows * TOPK // (3 * experts))
    position = lax.axis_index("tp")
    gathered = (
        lax.all_gather(w_query, "fsdp", axis=0, tiled=True),
        lax.all_gather(w_key, "fsdp", axis=0, tiled=True),
        lax.all_gather(w_value, "fsdp", axis=0, tiled=True),
        lax.all_gather(w_out, "fsdp", axis=1, tiled=True),
        lax.all_gather(w_shared_gate, "fsdp", axis=0, tiled=True),
        lax.all_gather(w_shared_up, "fsdp", axis=0, tiled=True),
        lax.all_gather(w_shared_down, "fsdp", axis=1, tiled=True),
        lax.all_gather(w_router, "fsdp", axis=0, tiled=True),
        lax.all_gather(gain_attn, "fsdp", axis=0, tiled=True),
        lax.all_gather(gain_ffn, "fsdp", axis=0, tiled=True),
    )
    (
        full_query,
        full_key,
        full_value,
        full_out,
        full_sgate,
        full_sup,
        full_sdown,
        full_router,
        gain_one_low,
        gain_two_low,
    ) = gathered
    first_norm_gain = gain_one_low.astype(jnp.float32)
    second_norm_gain = gain_two_low.astype(jnp.float32)
    group_tokens, group_cot = (
        lax.all_gather(tokens_in, "tp", axis=0, tiled=True),
        lax.all_gather(cotangent, "tp", axis=0, tiled=True),
    )
    residual = group_tokens.astype(jnp.float32)
    upstream = group_cot.astype(jnp.float32)
    scale_one = rms_scale(residual)
    normed_one = residual * scale_one
    attn_input = (normed_one * first_norm_gain).astype(jnp.bfloat16)
    heads_local = full_query.shape[1] // HEAD_SIZE
    kv_local = full_key.shape[1] // HEAD_SIZE
    tokens_per_group = QUERY_HEADS // KEY_VALUE_HEADS
    rotary_cosine, rotary_sine = rotary_tables(seq_rows)
    query_rot = (
        apply_rotary(
            product(attn_input, full_query).reshape(seq_rows, heads_local, HEAD_SIZE),
            rotary_cosine,
            rotary_sine,
        )
        .astype(jnp.bfloat16)
        .reshape(seq_rows, kv_local, tokens_per_group, HEAD_SIZE)
    )
    rotated_key = apply_rotary(
        product(attn_input, full_key).reshape(seq_rows, kv_local, HEAD_SIZE),
        rotary_cosine,
        rotary_sine,
    ).astype(jnp.bfloat16)
    value_low = (
        product(attn_input, full_value).astype(jnp.bfloat16).reshape(seq_rows, kv_local, HEAD_SIZE)
    )
    order_ids = jnp.arange(seq_rows)
    allowed = (doc_ids[:, None] == doc_ids[None, :]) & (order_ids[:, None] >= order_ids[None, :])
    scores = attention_scores(query_rot, rotated_key, allowed)
    top_score = jnp.max(scores, axis=-1, keepdims=True)
    weights = jnp.exp(scores - top_score)
    weight_sum = jnp.sum(weights, axis=-1, keepdims=True)
    log_total = top_score + jnp.log(weight_sum)
    probs_low = (weights / weight_sum).astype(jnp.bfloat16)
    heads_out = (
        jnp.einsum("gjqk,kgd->qgjd", probs_low, value_low, preferred_element_type=jnp.float32)
        .astype(jnp.bfloat16)
        .reshape(seq_rows, heads_local * HEAD_SIZE)
    )
    attn_branch = lax.psum(product(heads_out, full_out), "tp")
    middle = residual + attn_branch
    scale_two = rms_scale(middle)
    normed_two = middle * scale_two
    ffn_input = (normed_two * second_norm_gain).astype(jnp.bfloat16)
    logits = product(ffn_input, full_router)
    chosen = routes[:, :, None] == jnp.arange(experts, dtype=jnp.int32)[None, None, :]
    picked = jnp.sum(jnp.where(chosen, logits[:, None, :], 0.0), axis=-1)
    top_pick = jnp.max(picked, axis=-1, keepdims=True)
    gate_exp = jnp.exp(picked - top_pick)
    gate_values = gate_exp / jnp.sum(gate_exp, axis=-1, keepdims=True)
    shared_gate = product(ffn_input, full_sgate)
    shared_up = product(ffn_input, full_sup)
    shared_act = smooth_gate(shared_gate)
    shared_hidden = (shared_act * shared_up).astype(jnp.bfloat16)
    ffn_part = product(shared_hidden, full_sdown)
    flat_routes = routes.reshape(-1)
    onehot = (flat_routes[:, None] == jnp.arange(experts, dtype=jnp.int32)[None, :]).astype(
        jnp.int32
    )
    earlier = jnp.cumsum(onehot, axis=0) - onehot
    target = flat_routes * capacity + jnp.sum(earlier * onehot, axis=1)
    source = (
        jnp.full((experts * capacity,), -1, jnp.int32)
        .at[target]
        .set(jnp.arange(seq_rows * TOPK, dtype=jnp.int32))
    )
    filled = (source >= 0)[:, None]
    safe_source = jnp.maximum(source, 0)
    zero_low = jnp.zeros((), jnp.bfloat16)
    send_rows = jnp.where(filled, ffn_input[safe_source // TOPK], zero_low).reshape(
        experts, capacity, model_width
    )
    gated_cot = (
        (gate_values[:, :, None] * upstream[:, None, :])
        .astype(jnp.bfloat16)
        .reshape(seq_rows * TOPK, model_width)
    )
    send_grads = jnp.where(filled, gated_cot[safe_source], zero_low).reshape(
        experts, capacity, model_width
    )
    arrived = lax.all_to_all(send_rows, "fsdp", split_axis=0, concat_axis=0, tiled=True)
    slot_count = arrived.shape[1]
    grouped = arrived.reshape(sources, local_experts, slot_count, model_width)
    gate_pre = jnp.einsum(
        "sjcd,jdf->sjcf", grouped, w_expert_gate, preferred_element_type=jnp.float32
    )
    up_pre = jnp.einsum("sjcd,jdf->sjcf", grouped, w_expert_up, preferred_element_type=jnp.float32)
    hidden = (smooth_gate(gate_pre) * up_pre).astype(jnp.bfloat16)
    result = jnp.einsum(
        "sjcf,jfd->sjcd", hidden, w_expert_down, preferred_element_type=jnp.float32
    ).astype(jnp.bfloat16)
    half_width = gate_pre.shape[-1]
    expert_out = result.reshape(experts, slot_count, model_width)
    gate_keep = gate_pre.reshape(experts, slot_count, half_width)
    up_keep = up_pre.reshape(experts, slot_count, half_width)
    returned = lax.all_to_all(expert_out, "fsdp", split_axis=0, concat_axis=0, tiled=True)
    picked_rows = (
        returned.reshape(experts * capacity, model_width)[target]
        .reshape(seq_rows, TOPK, model_width)
        .astype(jnp.float32)
    )
    ffn_part = ffn_part + jnp.sum(gate_values[:, :, None] * picked_rows, axis=1)
    ffn_sum = lax.psum_scatter(
        ffn_part.astype(jnp.bfloat16), "tp", scatter_dimension=0, tiled=True
    ).astype(jnp.float32)
    middle_own = lax.dynamic_slice_in_dim(middle, position * own_rows, own_rows, 0)
    block_out = (middle_own + ffn_sum).astype(jnp.bfloat16)
    gate_grad = lax.psum(jnp.sum(upstream[:, None, :] * picked_rows, axis=-1), "tp")
    arrived_grads = lax.all_to_all(send_grads, "fsdp", split_axis=0, concat_axis=0, tiled=True)
    half_width = gate_keep.shape[-1]
    grad_rows = arrived_grads.reshape(sources, local_experts, capacity, model_width)
    input_rows = arrived.reshape(sources, local_experts, capacity, model_width)
    gate_pre = gate_keep.reshape(sources, local_experts, capacity, half_width)
    up_pre = up_keep.reshape(sources, local_experts, capacity, half_width)
    expert_act = smooth_gate(gate_pre)
    expert_hidden = (expert_act * up_pre).astype(jnp.bfloat16)
    hidden_grad = jnp.einsum(
        "sjcd,jfd->sjcf", grad_rows, w_expert_down, preferred_element_type=jnp.float32
    )
    grad_expert_down = jnp.einsum(
        "sjcf,sjcd->jfd", expert_hidden, grad_rows, preferred_element_type=jnp.float32
    )
    gate_low = (hidden_grad * up_pre * smooth_slope(gate_pre)).astype(jnp.bfloat16)
    up_low = (hidden_grad * expert_act).astype(jnp.bfloat16)
    grad_expert_gate = jnp.einsum(
        "sjcd,sjcf->jdf", input_rows, gate_low, preferred_element_type=jnp.float32
    )
    grad_expert_up = jnp.einsum(
        "sjcd,sjcf->jdf", input_rows, up_low, preferred_element_type=jnp.float32
    )
    row_grads = jnp.einsum(
        "sjcf,jdf->sjcd", gate_low, w_expert_gate, preferred_element_type=jnp.float32
    ) + jnp.einsum("sjcf,jdf->sjcd", up_low, w_expert_up, preferred_element_type=jnp.float32)
    row_grads = row_grads.astype(jnp.bfloat16).reshape(experts, capacity, model_width)
    back_rows = lax.all_to_all(row_grads, "fsdp", split_axis=0, concat_axis=0, tiled=True)
    input_grad = jnp.sum(
        back_rows.reshape(experts * capacity, model_width)[target]
        .reshape(seq_rows, TOPK, model_width)
        .astype(jnp.float32),
        axis=1,
    )
    shared_hidden_grad = times_transposed(group_cot, full_sdown)
    grad_shared_down = transposed_times(shared_hidden, group_cot)
    sgate_low = (shared_hidden_grad * shared_up * smooth_slope(shared_gate)).astype(jnp.bfloat16)
    sup_low = (shared_hidden_grad * shared_act).astype(jnp.bfloat16)
    grad_shared_gate = transposed_times(ffn_input, sgate_low)
    grad_shared_up = transposed_times(ffn_input, sup_low)
    input_grad = (
        input_grad + times_transposed(sgate_low, full_sgate) + times_transposed(sup_low, full_sup)
    )
    input_grad = lax.psum(input_grad, "tp")
    pick_grad = gate_values * (gate_grad - jnp.sum(gate_values * gate_grad, axis=-1, keepdims=True))
    logit_low = jnp.sum(jnp.where(chosen, pick_grad[:, :, None], 0.0), axis=1).astype(jnp.bfloat16)
    grad_router = transposed_times(ffn_input, logit_low)
    input_grad = input_grad + times_transposed(logit_low, full_router)
    grad_gain_ffn = jnp.sum(input_grad * normed_two, axis=0)
    middle_grad = upstream + norm_back(input_grad, normed_two, scale_two, second_norm_gain)
    attn_grad_low = middle_grad.astype(jnp.bfloat16)
    grad_out = transposed_times(heads_out, attn_grad_low)
    heads_grad = (
        times_transposed(attn_grad_low, full_out)
        .astype(jnp.bfloat16)
        .reshape(seq_rows, kv_local, tokens_per_group, HEAD_SIZE)
    )
    again_scores = attention_scores(query_rot, rotated_key, allowed)
    attn_probs = jnp.exp(again_scores - log_total)
    probs_grad = jnp.einsum(
        "qgjd,kgd->gjqk", heads_grad, value_low, preferred_element_type=jnp.float32
    )
    value_grad = (
        jnp.einsum(
            "gjqk,qgjd->kgd",
            attn_probs.astype(jnp.bfloat16),
            heads_grad,
            preferred_element_type=jnp.float32,
        )
        .astype(jnp.bfloat16)
        .reshape(seq_rows, kv_local * HEAD_SIZE)
    )
    score_low = (
        attn_probs * (probs_grad - jnp.sum(attn_probs * probs_grad, axis=-1, keepdims=True))
    ).astype(jnp.bfloat16)
    query_grad = jnp.einsum(
        "gjqk,kgd->qgjd", score_low, rotated_key, preferred_element_type=jnp.float32
    ) * HEAD_SIZE ** (-0.5)
    key_grad = jnp.einsum(
        "gjqk,qgjd->kgd", score_low, query_rot, preferred_element_type=jnp.float32
    ) * HEAD_SIZE ** (-0.5)
    query_low = (
        apply_rotary(
            query_grad.reshape(seq_rows, heads_local, HEAD_SIZE), rotary_cosine, -rotary_sine
        )
        .astype(jnp.bfloat16)
        .reshape(seq_rows, heads_local * HEAD_SIZE)
    )
    key_low = (
        apply_rotary(key_grad, rotary_cosine, -rotary_sine)
        .astype(jnp.bfloat16)
        .reshape(seq_rows, kv_local * HEAD_SIZE)
    )
    grad_query = transposed_times(attn_input, query_low)
    grad_key = transposed_times(attn_input, key_low)
    grad_value = transposed_times(attn_input, value_grad)
    attn_in_grad = (
        times_transposed(query_low, full_query)
        + times_transposed(key_low, full_key)
        + times_transposed(value_grad, full_value)
    )
    attn_in_grad = lax.psum(attn_in_grad.astype(jnp.bfloat16), "tp").astype(jnp.float32)
    grad_gain_attn = jnp.sum(attn_in_grad * normed_one, axis=0)
    token_grad = middle_grad + norm_back(attn_in_grad, normed_one, scale_one, first_norm_gain)
    grad_tokens = lax.dynamic_slice_in_dim(token_grad, position * own_rows, own_rows, 0)
    everything = (
        lax.psum_scatter(grad_query, "fsdp", scatter_dimension=0, tiled=True),
        lax.psum_scatter(grad_key, "fsdp", scatter_dimension=0, tiled=True),
        lax.psum_scatter(grad_value, "fsdp", scatter_dimension=0, tiled=True),
        lax.psum_scatter(grad_out, "fsdp", scatter_dimension=1, tiled=True),
        lax.psum_scatter(grad_gain_attn, "fsdp", scatter_dimension=0, tiled=True),
        lax.psum_scatter(grad_shared_gate, "fsdp", scatter_dimension=0, tiled=True),
        lax.psum_scatter(grad_shared_up, "fsdp", scatter_dimension=0, tiled=True),
        lax.psum_scatter(grad_shared_down, "fsdp", scatter_dimension=1, tiled=True),
        lax.psum_scatter(grad_router, "fsdp", scatter_dimension=0, tiled=True),
        lax.psum_scatter(grad_gain_ffn, "fsdp", scatter_dimension=0, tiled=True),
    )
    attn_grads = everything[:5]
    ffn_grads = everything[5:]
    return (
        block_out,
        grad_tokens,
        attn_grads[4],
        attn_grads[0],
        attn_grads[1],
        attn_grads[2],
        attn_grads[3],
        ffn_grads[4],
        ffn_grads[3],
        ffn_grads[0],
        ffn_grads[1],
        ffn_grads[2],
        grad_expert_gate,
        grad_expert_up,
        grad_expert_down,
    )


GROUP_IDS = ((0, 8), (4, 12), (2, 10), (5, 13), (1, 9), (6, 14), (3, 11), (7, 15))


def hop(values, bit):
    count = lax.axis_size("fsdp")
    return lax.ppermute(values, "fsdp", [(i, i ^ bit) for i in range(count)])


def swap(values):
    return lax.ppermute(values, "tp", [(0, 1), (1, 0)])


def join(*parts):
    return jnp.concatenate(parts, axis=0)


def spread(block):
    far = hop(block, 8)
    near = hop(block, 4)
    cross = hop(block, 12)
    even0, odd0 = join(block, far), join(near, cross)
    even1, odd1 = hop(even0, 2), hop(odd0, 1)
    even2, odd2 = hop(even0, 1), hop(odd0, 2)
    even3, odd3 = hop(even1, 1), hop(odd1, 2)
    return even0, odd0, even1, odd1, even2, odd2, even3, odd3


def plus(left, right):
    return (left.astype(jnp.float32) + right.astype(jnp.float32)).astype(jnp.bfloat16)


def collect(groups):
    even0, odd0, even1, odd1, even2, odd2, even3, odd3 = groups
    even1 = plus(even1, hop(even3, 1))
    odd1 = plus(odd1, hop(odd3, 2))
    even0 = plus(even0, hop(even2, 1))
    odd0 = plus(odd0, hop(odd2, 2))
    even0 = plus(even0, hop(even1, 2))
    odd0 = plus(odd0, hop(odd1, 1))
    rows = even0.shape[0] // 2
    far = hop(even0[rows:], 8)
    near = hop(odd0[:rows], 4)
    cross = hop(odd0[rows:], 12)
    return (
        even0[:rows].astype(jnp.float32)
        + far.astype(jnp.float32)
        + near.astype(jnp.float32)
        + cross.astype(jnp.float32)
    )


def in_order(groups, me):
    rows = groups[0].shape[0] // 2
    whole = jnp.zeros((rows * 2 * len(groups), groups[0].shape[1]), groups[0].dtype)
    for ids, group in zip(GROUP_IDS, groups, strict=True):
        for place, index in enumerate(ids):
            whole = lax.dynamic_update_slice_in_dim(
                whole, group[place * rows : (place + 1) * rows], (me ^ index) * rows, 0
            )
    return whole


def in_groups(whole, me):
    rows = whole.shape[0] // (2 * len(GROUP_IDS))
    return [
        join(
            *(
                lax.dynamic_slice_in_dim(whole, (me ^ index) * rows, rows, 0).astype(jnp.bfloat16)
                for index in ids
            )
        )
        for ids in GROUP_IDS
    ]


def expert_kernel(
    first,
    own_ref,
    other_ref,
    cot_own_ref,
    cot_other_ref,
    place_ref,
    gate_ref,
    w_gate_ref,
    w_up_ref,
    w_down_ref,
    shared_in_ref,
    shared_out_ref,
    *rest,
):
    if first:
        outs = rest
    else:
        shared_sum_ref = rest[0]
        outs = rest[6:]
    (
        shared_grad_ref,
        rows_ref,
        dy_ref,
        hidden_ref,
        dgate_ref,
        dup_ref,
        back_own_ref,
        back_other_ref,
        out_own_ref,
        out_other_ref,
        pick_ref,
        cot_rows,
        back_sum,
        out_sum,
        pick_sum,
        gate_column,
    ) = outs
    step = pl.program_id(0)
    slots = own_ref.shape[0]

    def chooser(part):
        numbers = lax.broadcasted_iota(jnp.int32, (slots, slots), 0).astype(jnp.float32)
        return numbers == place_ref[0, part : part + 1, :]

    @pl.when(step == 0)
    def start():
        chosen = [chooser(0), chooser(1)]
        low = [c.astype(jnp.bfloat16) for c in chosen]
        rows_ref[...] = (product(low[0], own_ref[...]) + product(low[1], other_ref[...])).astype(
            jnp.bfloat16
        )
        cot = product(low[0], cot_own_ref[...]) + product(low[1], cot_other_ref[...])
        cot_rows[...] = cot.astype(jnp.bfloat16)
        gates = sum(
            jnp.sum(
                jnp.where(chosen[part], gate_ref[0, part : part + 1, :], 0.0),
                axis=1,
                keepdims=True,
            )
            for part in range(2)
        )
        gate_column[...] = gates
        dy_ref[...] = (gates * cot).astype(jnp.bfloat16)
        back_sum[...] = jnp.zeros_like(back_sum)
        out_sum[...] = jnp.zeros_like(out_sum)
        pick_sum[...] = jnp.zeros_like(pick_sum)

    gates = gate_column[...]
    gate_pre = product(rows_ref[...], w_gate_ref[0])
    up_pre = product(rows_ref[...], w_up_ref[0])
    cot_hidden = times_transposed(cot_rows[...], w_down_ref[0])
    sigmoid = 1.0 / (1.0 + jnp.exp(-gate_pre))
    act = gate_pre * sigmoid
    hidden = (act * up_pre).astype(jnp.bfloat16)
    hidden_grad = gates * cot_hidden
    gate_low = (hidden_grad * up_pre * (sigmoid * (1.0 + gate_pre * (1.0 - sigmoid)))).astype(
        jnp.bfloat16
    )
    up_low = (hidden_grad * act).astype(jnp.bfloat16)
    hidden_ref[...] = hidden
    dgate_ref[...] = gate_low
    dup_ref[...] = up_low
    pick_sum[...] += jnp.sum(hidden.astype(jnp.float32) * cot_hidden, axis=1, keepdims=True)
    back_sum[...] += times_transposed(gate_low, w_gate_ref[0]) + times_transposed(
        up_low, w_up_ref[0]
    )
    out_sum[...] += product(hidden, w_down_ref[0])

    @pl.when(step == pl.num_programs(0) - 1)
    def finish():
        back_rows = back_sum[...].astype(jnp.bfloat16)
        out_rows = (gates * out_sum[...]).astype(jnp.bfloat16)
        picks = pick_sum[...]
        total = None
        half = shared_out_ref.shape[0]
        for part, (tok_ref, cot_ref, back_ref, out_ref) in enumerate(
            (
                (own_ref, cot_own_ref, back_own_ref, out_own_ref),
                (other_ref, cot_other_ref, back_other_ref, out_other_ref),
            )
        ):
            chosen = chooser(part)
            pick_ref[0, part : part + 1, :] = jnp.sum(
                jnp.where(chosen, picks, 0.0), axis=0, keepdims=True
            )
            low = chosen.astype(jnp.bfloat16)
            both = product(tok_ref[...], shared_in_ref[...])
            pre, up = both[:, :half], both[:, half:]
            hid_grad = times_transposed(cot_ref[...], shared_out_ref[...])
            sig = 1.0 / (1.0 + jnp.exp(-pre))
            sact = pre * sig
            shid = (sact * up).astype(jnp.bfloat16)
            sboth = jnp.concatenate(
                [hid_grad * up * (sig * (1.0 + pre * (1.0 - sig))), hid_grad * sact], axis=1
            ).astype(jnp.bfloat16)
            back_ref[...] = (
                transposed_times(low, back_rows) + times_transposed(sboth, shared_in_ref[...])
            ).astype(jnp.bfloat16)
            out_ref[...] = (
                transposed_times(low, out_rows) + product(shid, shared_out_ref[...])
            ).astype(jnp.bfloat16)
            grads = jnp.concatenate(
                [
                    transposed_times(sboth, tok_ref[...]),
                    transposed_times(shid, cot_ref[...]),
                ],
                axis=0,
            )
            total = grads if total is None else total + grads
        if first:
            shared_grad_ref[...] = total
        else:
            shared_grad_ref[...] = shared_sum_ref[...] + total


def expert_call(number, tokens, cots, places, gates, weights, kept):
    own, other = tokens
    cot_own, cot_other = cots
    w_gate, w_up, w_down, shared_in, shared_out = weights
    slots, width = own.shape
    hidden = w_gate.shape[2]
    tile = 256
    total = slots * len(GROUP_IDS)
    first = kept is None

    def whole(shape):
        return pl.BlockSpec(shape, lambda h: (0,) * len(shape), pipeline_mode=pl.Buffered(1))

    def rows_block(columns):
        return pl.BlockSpec((slots, columns), lambda h: (number, 0))

    def tile_block():
        return pl.BlockSpec((slots, tile), lambda h: (number, h))

    def fixed(shape):
        return pl.BlockSpec(shape, lambda h: (0,) * len(shape))

    shared_rows = shared_in.shape[1] + shared_out.shape[0]
    in_specs = [
        whole((slots, width)),
        whole((slots, width)),
        whole((slots, width)),
        whole((slots, width)),
        pl.BlockSpec((1, 2, slots), lambda h: (number, 0, 0)),
        pl.BlockSpec((1, 2, slots), lambda h: (number, 0, 0)),
        pl.BlockSpec((1, width, tile), lambda h: (0, 0, h)),
        pl.BlockSpec((1, width, tile), lambda h: (0, 0, h)),
        pl.BlockSpec((1, tile, width), lambda h: (0, h, 0)),
        whole(shared_in.shape),
        whole(shared_out.shape),
    ]
    operands = [own, other, cot_own, cot_other, places, gates, w_gate, w_up, w_down]
    operands += [shared_in, shared_out]
    aliases = {}
    if not first:
        in_specs += [whole((shared_rows, width))] + [pl.BlockSpec(memory_space=pl.ANY)] * 5
        aliases = {len(operands) + i: i for i in range(6)}
        operands += list(kept)
    low = jnp.bfloat16
    out_shape = [
        jax.ShapeDtypeStruct((shared_rows, width), jnp.float32),
        jax.ShapeDtypeStruct((total, width), low),
        jax.ShapeDtypeStruct((total, width), low),
        jax.ShapeDtypeStruct((total, hidden), low),
        jax.ShapeDtypeStruct((total, hidden), low),
        jax.ShapeDtypeStruct((total, hidden), low),
        jax.ShapeDtypeStruct((slots, width), low),
        jax.ShapeDtypeStruct((slots, width), low),
        jax.ShapeDtypeStruct((slots, width), low),
        jax.ShapeDtypeStruct((slots, width), low),
        jax.ShapeDtypeStruct((1, 2, slots), jnp.float32),
    ]
    out_specs = [
        fixed((shared_rows, width)),
        rows_block(width),
        rows_block(width),
        tile_block(),
        tile_block(),
        tile_block(),
        fixed((slots, width)),
        fixed((slots, width)),
        fixed((slots, width)),
        fixed((slots, width)),
        fixed((1, 2, slots)),
    ]
    results = pl.pallas_call(
        lambda *refs: expert_kernel(first, *refs),
        grid=(hidden // tile,),
        in_specs=in_specs,
        out_specs=out_specs,
        out_shape=out_shape,
        scratch_shapes=[
            pltpu.VMEM((slots, width), low),
            pltpu.VMEM((slots, width), jnp.float32),
            pltpu.VMEM((slots, width), jnp.float32),
            pltpu.VMEM((slots, 1), jnp.float32),
            pltpu.VMEM((slots, 1), jnp.float32),
        ],
        input_output_aliases=aliases,
        compiler_params=pltpu.CompilerParams(
            dimension_semantics=("arbitrary",), vmem_limit_bytes=60 * 1024 * 1024
        ),
        cost_estimate=pl.CostEstimate(
            flops=2 * slots * width * (6 * hidden + 2 * slots + 6 * slots),
            bytes_accessed=24 * 1024 * 1024,
            transcendentals=slots * hidden,
        ),
        name="expert_pass",
    )(*operands)
    return results[:6], results[6:8], results[8:10], results[10]


def gathered_shards(
    tokens_in,
    cotangent,
    doc_ids,
    routes,
    gain_attn,
    w_query,
    w_key,
    w_value,
    w_out,
    gain_ffn,
    w_router,
    w_shared_gate,
    w_shared_up,
    w_shared_down,
    w_expert_gate,
    w_expert_up,
    w_expert_down,
):
    low = jnp.bfloat16
    own_rows, width = tokens_in.shape
    seq_rows = doc_ids.shape[0]
    experts = w_router.shape[1]
    sources = lax.axis_size("fsdp")
    capacity = max(2, 4 * seq_rows * TOPK // (3 * experts))
    me = lax.axis_index("fsdp")
    side = lax.axis_index("tp")
    relative = jnp.arange(sources, dtype=jnp.int32) ^ me
    query_width, kv_width = w_query.shape[1], w_key.shape[1]
    heads_local, kv_local = query_width // HEAD_SIZE, kv_width // HEAD_SIZE
    per_kv = QUERY_HEADS // KEY_VALUE_HEADS

    small = jnp.concatenate([gain_attn[:, None], gain_ffn[:, None], w_router], axis=1)
    small_width = small.shape[1]
    small = jnp.pad(small, ((0, 0), (0, -small_width % 128)))
    packed = jnp.concatenate([w_query, w_key, w_value, small], axis=1)
    full_in = in_order(spread(packed), me)
    qkv_width = query_width + 2 * kv_width
    full_qkv = full_in[:, :qkv_width]
    gain_one = full_in[:, qkv_width].astype(jnp.float32)
    gain_two = full_in[:, qkv_width + 1].astype(jnp.float32)
    full_router = full_in[:, qkv_width + 2 : qkv_width + small_width]
    full_out = in_order(spread(w_out.T), me)

    slice_width = w_shared_gate.shape[1] // sources
    pad_width = -slice_width % 128
    shards_in = jnp.concatenate(
        [
            jnp.pad(
                part.reshape(part.shape[0], sources, slice_width), ((0, 0), (0, 0), (0, pad_width))
            )
            for part in (w_shared_gate, w_shared_up, w_shared_down.T)
        ],
        axis=2,
    )
    shared_all = lax.all_to_all(
        shards_in.transpose(1, 0, 2), "fsdp", split_axis=0, concat_axis=0, tiled=True
    ).reshape(width, 3 * (slice_width + pad_width))
    wide = slice_width + pad_width
    shared_in = shared_all[:, : 2 * wide]
    shared_out = shared_all[:, 2 * wide :].T

    cot_groups = spread(cotangent)
    cot_pairs = [(group, swap(group)) for group in cot_groups]

    tokens_all = join(tokens_in, swap(tokens_in))
    residual = tokens_all.astype(jnp.float32)
    scale_one = rms_scale(residual)
    normed_one = residual * scale_one
    attn_input = (normed_one * gain_one).astype(low)
    turn = side * own_rows
    rotary_cosine, rotary_sine = (jnp.roll(t, -turn, axis=0) for t in rotary_tables(seq_rows))
    order_ids = jnp.roll(jnp.arange(seq_rows), -turn)
    docs = jnp.roll(doc_ids, -turn)
    projected = product(attn_input, full_qkv)
    query_rot = (
        apply_rotary(
            projected[:, :query_width].reshape(seq_rows, heads_local, HEAD_SIZE),
            rotary_cosine,
            rotary_sine,
        )
        .astype(low)
        .reshape(seq_rows, kv_local, per_kv, HEAD_SIZE)
    )
    rotated_key = apply_rotary(
        projected[:, query_width : query_width + kv_width].reshape(seq_rows, kv_local, HEAD_SIZE),
        rotary_cosine,
        rotary_sine,
    ).astype(low)
    value_low = projected[:, query_width + kv_width :].astype(low)
    value_low = value_low.reshape(seq_rows, kv_local, HEAD_SIZE)
    allowed = (docs[:, None] == docs[None, :]) & (order_ids[:, None] >= order_ids[None, :])
    scores = attention_scores(query_rot, rotated_key, allowed)
    top_score = jnp.max(scores, axis=-1, keepdims=True)
    weights = jnp.exp(scores - top_score)
    attn_probs = weights / jnp.sum(weights, axis=-1, keepdims=True)
    probs_low = attn_probs.astype(low)
    heads_out = (
        jnp.einsum("gjqk,kgd->qgjd", probs_low, value_low, preferred_element_type=jnp.float32)
        .astype(low)
        .reshape(seq_rows, heads_local * HEAD_SIZE)
    )
    branch = times_transposed(heads_out, full_out)
    middle = tokens_in.astype(jnp.float32) + (branch[:own_rows] + swap(branch[own_rows:]))

    scale_two = rms_scale(middle)
    normed_two = middle * scale_two
    ffn_input = (normed_two * gain_two).astype(low)
    ffn_groups = spread(ffn_input)
    ffn_pairs = [(group, swap(group)) for group in ffn_groups]
    logits = product(ffn_input, full_router)
    own_routes = lax.dynamic_slice_in_dim(routes, turn, own_rows, 0)
    routed = jnp.any(
        own_routes[:, :, None] == jnp.arange(experts, dtype=jnp.int32)[None, None, :], axis=1
    )
    top_pick = jnp.max(jnp.where(routed, logits, -jnp.inf), axis=-1, keepdims=True)
    gate_exp = jnp.where(routed, jnp.exp(logits - top_pick), 0.0)
    gate_values = gate_exp / jnp.sum(gate_exp, axis=-1, keepdims=True)
    sent_gates = jnp.where(routed, gate_values, -1.0).T
    got_gates = lax.all_to_all(sent_gates, "fsdp", split_axis=0, concat_axis=0, tiled=True)
    got_gates = got_gates[relative]
    both_gates = jnp.stack([got_gates, swap(got_gates)], axis=1)
    flags = (both_gates >= 0.0).astype(low).reshape(sources, seq_rows)
    before = (jnp.arange(seq_rows)[:, None] < jnp.arange(seq_rows)[None, :]).astype(low)
    ranks = product(flags, before).reshape(both_gates.shape)
    ids = jnp.asarray(GROUP_IDS)
    offsets = jnp.arange(2, dtype=jnp.float32)[None, :, None, None] * capacity
    places = jnp.where(both_gates[ids] >= 0.0, ranks[ids] + offsets, -1.0)
    places = places.transpose(0, 2, 1, 3).reshape(len(GROUP_IDS), 2, 2 * own_rows)
    gate_rows = both_gates[ids].transpose(0, 2, 1, 3).reshape(len(GROUP_IDS), 2, 2 * own_rows)

    expert_weights = (w_expert_gate, w_expert_up, w_expert_down, shared_in, shared_out)
    kept = None
    back_pairs, out_pairs, picks = [], [], []
    for number in range(len(GROUP_IDS)):
        kept, back, out, pick = expert_call(
            number,
            ffn_pairs[number],
            cot_pairs[number],
            places,
            gate_rows,
            expert_weights,
            kept,
        )
        back_pairs.append(back)
        out_pairs.append(out)
        picks.append(pick)
    shared_grads, slot_rows, slot_dy, slot_hidden, slot_dgate, slot_dup = kept
    input_grad = collect([plus(own, swap(other)) for own, other in back_pairs])
    ffn_sum = collect([plus(own, swap(other)) for own, other in out_pairs])
    block_out = (middle + ffn_sum).astype(low)

    pick_groups = jnp.concatenate(picks, axis=0)
    pick_groups = pick_groups.reshape(len(GROUP_IDS), 2, 2, own_rows)
    pick_groups = pick_groups[:, 0] + swap(pick_groups[:, 1])
    pick_blocks = jnp.zeros((sources, own_rows), jnp.float32)
    pick_blocks = pick_blocks.at[ids.reshape(-1)].set(pick_groups.reshape(sources, own_rows))
    gate_grad = lax.all_to_all(
        pick_blocks[relative], "fsdp", split_axis=0, concat_axis=0, tiled=True
    ).T

    grad_expert_down = transposed_times(slot_hidden, slot_dy)[None]
    grad_expert_gate = transposed_times(slot_rows, slot_dgate)[None]
    grad_expert_up = transposed_times(slot_rows, slot_dup)[None]

    shared_back = shared_grads.astype(low).T.reshape(sources, width // sources, 3 * wide)
    shared_back = lax.all_to_all(shared_back, "fsdp", split_axis=0, concat_axis=0, tiled=True)
    shared_back = shared_back.transpose(1, 0, 2).astype(jnp.float32)
    grad_shared_gate, grad_shared_up, grad_shared_down = (
        shared_back[:, :, i * wide : i * wide + slice_width].reshape(width // sources, -1)
        for i in range(3)
    )
    grad_shared_down = grad_shared_down.T

    pick_grad = gate_values * (gate_grad - jnp.sum(gate_values * gate_grad, axis=-1, keepdims=True))
    logit_low = jnp.where(routed, pick_grad, 0.0).astype(low)
    grad_router = transposed_times(ffn_input, logit_low)
    input_grad = input_grad + times_transposed(logit_low, full_router)
    grad_gain_ffn = jnp.sum(input_grad * normed_two, axis=0)
    middle_grad = cotangent.astype(jnp.float32) + norm_back(
        input_grad, normed_two, scale_two, gain_two
    )
    attn_grad_own = middle_grad.astype(low)
    attn_grad_low = join(attn_grad_own, swap(attn_grad_own))

    grad_out = transposed_times(attn_grad_low, heads_out)
    heads_grad = (
        product(attn_grad_low, full_out).astype(low).reshape(seq_rows, kv_local, per_kv, HEAD_SIZE)
    )
    probs_grad = jnp.einsum(
        "qgjd,kgd->gjqk", heads_grad, value_low, preferred_element_type=jnp.float32
    )
    value_grad = (
        jnp.einsum("gjqk,qgjd->kgd", probs_low, heads_grad, preferred_element_type=jnp.float32)
        .astype(low)
        .reshape(seq_rows, kv_width)
    )
    score_low = (
        attn_probs * (probs_grad - jnp.sum(attn_probs * probs_grad, axis=-1, keepdims=True))
    ).astype(low)
    query_grad = jnp.einsum(
        "gjqk,kgd->qgjd", score_low, rotated_key, preferred_element_type=jnp.float32
    ) * HEAD_SIZE ** (-0.5)
    key_grad = jnp.einsum(
        "gjqk,qgjd->kgd", score_low, query_rot, preferred_element_type=jnp.float32
    ) * HEAD_SIZE ** (-0.5)
    query_low = (
        apply_rotary(
            query_grad.reshape(seq_rows, heads_local, HEAD_SIZE), rotary_cosine, -rotary_sine
        )
        .astype(low)
        .reshape(seq_rows, query_width)
    )
    key_low = (
        apply_rotary(key_grad, rotary_cosine, -rotary_sine).astype(low).reshape(seq_rows, kv_width)
    )
    qkv_low = jnp.concatenate([query_low, key_low, value_grad], axis=1)
    grad_qkv = transposed_times(attn_input, qkv_low)
    attn_in_grad = times_transposed(qkv_low, full_qkv).astype(low)
    attn_in_grad = attn_in_grad[:own_rows].astype(jnp.float32) + swap(
        attn_in_grad[own_rows:]
    ).astype(jnp.float32)
    normed_own, scale_own = normed_one[:own_rows], scale_one[:own_rows]
    grad_gain_attn = jnp.sum(attn_in_grad * normed_own, axis=0)
    grad_tokens = middle_grad + norm_back(attn_in_grad, normed_own, scale_own, gain_one)

    small_grads = jnp.concatenate(
        [grad_gain_attn[:, None], grad_gain_ffn[:, None], grad_router], axis=1
    )
    small_grads = small_grads + swap(small_grads)
    small_grads = jnp.pad(small_grads, ((0, 0), (0, -small_width % 128)))
    out_sum = collect(in_groups(grad_out, me))
    in_sum = collect(in_groups(jnp.concatenate([grad_qkv, small_grads], axis=1), me))
    small_sum = in_sum[:, qkv_width:]
    return (
        block_out,
        grad_tokens,
        small_sum[:, 0],
        in_sum[:, :query_width],
        in_sum[:, query_width : query_width + kv_width],
        in_sum[:, query_width + kv_width : qkv_width],
        out_sum.T,
        small_sum[:, 1],
        small_sum[:, 2:small_width],
        grad_shared_gate,
        grad_shared_up,
        grad_shared_down,
        grad_expert_gate,
        grad_expert_up,
        grad_expert_down,
    )


def solution(mesh):
    wide = mesh.shape["fsdp"] == 16 and mesh.shape["tp"] == 2
    return jax.shard_map(
        gathered_shards if wide else shards,
        mesh=mesh,
        in_specs=(
            P(("fsdp", "tp"), None),
            P(("fsdp", "tp"), None),
            P("fsdp"),
            P("fsdp", None),
            P("fsdp"),
            P("fsdp", "tp"),
            P("fsdp", "tp"),
            P("fsdp", "tp"),
            P("tp", "fsdp"),
            P("fsdp"),
            P("fsdp", None),
            P("fsdp", "tp"),
            P("fsdp", "tp"),
            P("tp", "fsdp"),
            P("fsdp", None, "tp"),
            P("fsdp", None, "tp"),
            P("fsdp", "tp", None),
        ),
        out_specs=(
            P(("fsdp", "tp"), None),
            P(("fsdp", "tp"), None),
            P("fsdp"),
            P("fsdp", "tp"),
            P("fsdp", "tp"),
            P("fsdp", "tp"),
            P("tp", "fsdp"),
            P("fsdp"),
            P("fsdp", None),
            P("fsdp", "tp"),
            P("fsdp", "tp"),
            P("tp", "fsdp"),
            P("fsdp", None, "tp"),
            P("fsdp", None, "tp"),
            P("fsdp", "tp", None),
        ),
        check_vma=False,
    )
```

```python
import jax
import jax.numpy as jnp
from jax import lax
from jax.experimental import pallas as pl
from jax.experimental.layout import Layout, with_layout_constraint
from jax.experimental.pallas import tpu as pltpu
from jax.sharding import PartitionSpec as P

QUERY_HEADS = 20
KEY_VALUE_HEADS = 4
HEAD_SIZE = 128
TOPK = 6


norm_eps = 1e-05
rope_base = 500000.0


def rotary_tables(length_total):
    half_width = HEAD_SIZE // 2
    inverse = 1.0 / rope_base ** (jnp.arange(half_width, dtype=jnp.float32) * (2.0 / HEAD_SIZE))
    angles = jnp.arange(length_total, dtype=jnp.float32)[:, None] * inverse[None, :]
    return (jnp.cos(angles), jnp.sin(angles))


def apply_rotary(values, rotary_cosine, rotary_sine):
    half_width = values.shape[-1] // 2
    first_half = values[..., :half_width]
    second_half = values[..., half_width:]
    cos_rows = rotary_cosine[:, None, :]
    sin_rows = rotary_sine[:, None, :]
    return jnp.concatenate(
        [
            first_half * cos_rows - second_half * sin_rows,
            second_half * cos_rows + first_half * sin_rows,
        ],
        axis=-1,
    )


def smooth_gate(values):
    return values / (1.0 + jnp.exp(-values))


def smooth_slope(values):
    sigmoid = 1.0 / (1.0 + jnp.exp(-values))
    return sigmoid * (1.0 + values * (1.0 - sigmoid))


def rms_scale(values):
    return lax.rsqrt(jnp.mean(values * values, axis=-1, keepdims=True) + norm_eps)


def norm_back(grad_in, normed, inv_rms, gain_vec):
    scaled = grad_in * gain_vec
    return inv_rms * (scaled - normed * jnp.mean(scaled * normed, axis=-1, keepdims=True))


def product(left_mat, right_mat):
    return jnp.dot(left_mat, right_mat, preferred_element_type=jnp.float32)


def times_transposed(left_mat, right_mat):
    return lax.dot_general(
        left_mat, right_mat, (((1,), (1,)), ((), ())), preferred_element_type=jnp.float32
    )


def transposed_times(left_mat, right_mat):
    return lax.dot_general(
        left_mat, right_mat, (((0,), (0,)), ((), ())), preferred_element_type=jnp.float32
    )


def attention_scores(query_rot, rotated_key, allowed):
    scores = jnp.einsum(
        "qgjd,kgd->gjqk", query_rot, rotated_key, preferred_element_type=jnp.float32
    ) * HEAD_SIZE ** (-0.5)
    return jnp.where(allowed, scores, -1e30)


def shards(
    tokens_in,
    cotangent,
    doc_ids,
    routes,
    gain_attn,
    w_query,
    w_key,
    w_value,
    w_out,
    gain_ffn,
    w_router,
    w_shared_gate,
    w_shared_up,
    w_shared_down,
    w_expert_gate,
    w_expert_up,
    w_expert_down,
):
    own_rows = tokens_in.shape[0]
    seq_rows = doc_ids.shape[0]
    model_width = tokens_in.shape[1]
    experts = w_router.shape[1]
    local_experts = w_expert_gate.shape[0]
    sources = experts // local_experts
    capacity = max(2, 4 * seq_rows * TOPK // (3 * experts))
    position = lax.axis_index("tp")
    gathered = (
        lax.all_gather(w_query, "fsdp", axis=0, tiled=True),
        lax.all_gather(w_key, "fsdp", axis=0, tiled=True),
        lax.all_gather(w_value, "fsdp", axis=0, tiled=True),
        lax.all_gather(w_out, "fsdp", axis=1, tiled=True),
        lax.all_gather(w_shared_gate, "fsdp", axis=0, tiled=True),
        lax.all_gather(w_shared_up, "fsdp", axis=0, tiled=True),
        lax.all_gather(w_shared_down, "fsdp", axis=1, tiled=True),
        lax.all_gather(w_router, "fsdp", axis=0, tiled=True),
        lax.all_gather(gain_attn, "fsdp", axis=0, tiled=True),
        lax.all_gather(gain_ffn, "fsdp", axis=0, tiled=True),
    )
    (
        full_query,
        full_key,
        full_value,
        full_out,
        full_sgate,
        full_sup,
        full_sdown,
        full_router,
        gain_one_low,
        gain_two_low,
    ) = gathered
    first_norm_gain = gain_one_low.astype(jnp.float32)
    second_norm_gain = gain_two_low.astype(jnp.float32)
    group_tokens, group_cot = (
        lax.all_gather(tokens_in, "tp", axis=0, tiled=True),
        lax.all_gather(cotangent, "tp", axis=0, tiled=True),
    )
    residual = group_tokens.astype(jnp.float32)
    upstream = group_cot.astype(jnp.float32)
    scale_one = rms_scale(residual)
    normed_one = residual * scale_one
    attn_input = (normed_one * first_norm_gain).astype(jnp.bfloat16)
    heads_local = full_query.shape[1] // HEAD_SIZE
    kv_local = full_key.shape[1] // HEAD_SIZE
    tokens_per_group = QUERY_HEADS // KEY_VALUE_HEADS
    rotary_cosine, rotary_sine = rotary_tables(seq_rows)
    query_rot = (
        apply_rotary(
            product(attn_input, full_query).reshape(seq_rows, heads_local, HEAD_SIZE),
            rotary_cosine,
            rotary_sine,
        )
        .astype(jnp.bfloat16)
        .reshape(seq_rows, kv_local, tokens_per_group, HEAD_SIZE)
    )
    rotated_key = apply_rotary(
        product(attn_input, full_key).reshape(seq_rows, kv_local, HEAD_SIZE),
        rotary_cosine,
        rotary_sine,
    ).astype(jnp.bfloat16)
    value_low = (
        product(attn_input, full_value).astype(jnp.bfloat16).reshape(seq_rows, kv_local, HEAD_SIZE)
    )
    order_ids = jnp.arange(seq_rows)
    allowed = (doc_ids[:, None] == doc_ids[None, :]) & (order_ids[:, None] >= order_ids[None, :])
    scores = attention_scores(query_rot, rotated_key, allowed)
    top_score = jnp.max(scores, axis=-1, keepdims=True)
    weights = jnp.exp(scores - top_score)
    weight_sum = jnp.sum(weights, axis=-1, keepdims=True)
    log_total = top_score + jnp.log(weight_sum)
    probs_low = (weights / weight_sum).astype(jnp.bfloat16)
    heads_out = (
        jnp.einsum("gjqk,kgd->qgjd", probs_low, value_low, preferred_element_type=jnp.float32)
        .astype(jnp.bfloat16)
        .reshape(seq_rows, heads_local * HEAD_SIZE)
    )
    attn_branch = lax.psum(product(heads_out, full_out), "tp")
    middle = residual + attn_branch
    scale_two = rms_scale(middle)
    normed_two = middle * scale_two
    ffn_input = (normed_two * second_norm_gain).astype(jnp.bfloat16)
    logits = product(ffn_input, full_router)
    chosen = routes[:, :, None] == jnp.arange(experts, dtype=jnp.int32)[None, None, :]
    picked = jnp.sum(jnp.where(chosen, logits[:, None, :], 0.0), axis=-1)
    top_pick = jnp.max(picked, axis=-1, keepdims=True)
    gate_exp = jnp.exp(picked - top_pick)
    gate_values = gate_exp / jnp.sum(gate_exp, axis=-1, keepdims=True)
    shared_gate = product(ffn_input, full_sgate)
    shared_up = product(ffn_input, full_sup)
    shared_act = smooth_gate(shared_gate)
    shared_hidden = (shared_act * shared_up).astype(jnp.bfloat16)
    ffn_part = product(shared_hidden, full_sdown)
    flat_routes = routes.reshape(-1)
    onehot = (flat_routes[:, None] == jnp.arange(experts, dtype=jnp.int32)[None, :]).astype(
        jnp.int32
    )
    earlier = jnp.cumsum(onehot, axis=0) - onehot
    target = flat_routes * capacity + jnp.sum(earlier * onehot, axis=1)
    source = (
        jnp.full((experts * capacity,), -1, jnp.int32)
        .at[target]
        .set(jnp.arange(seq_rows * TOPK, dtype=jnp.int32))
    )
    filled = (source >= 0)[:, None]
    safe_source = jnp.maximum(source, 0)
    zero_low = jnp.zeros((), jnp.bfloat16)
    send_rows = jnp.where(filled, ffn_input[safe_source // TOPK], zero_low).reshape(
        experts, capacity, model_width
    )
    gated_cot = (
        (gate_values[:, :, None] * upstream[:, None, :])
        .astype(jnp.bfloat16)
        .reshape(seq_rows * TOPK, model_width)
    )
    send_grads = jnp.where(filled, gated_cot[safe_source], zero_low).reshape(
        experts, capacity, model_width
    )
    arrived = lax.all_to_all(send_rows, "fsdp", split_axis=0, concat_axis=0, tiled=True)
    slot_count = arrived.shape[1]
    grouped = arrived.reshape(sources, local_experts, slot_count, model_width)
    gate_pre = jnp.einsum(
        "sjcd,jdf->sjcf", grouped, w_expert_gate, preferred_element_type=jnp.float32
    )
    up_pre = jnp.einsum("sjcd,jdf->sjcf", grouped, w_expert_up, preferred_element_type=jnp.float32)
    hidden = (smooth_gate(gate_pre) * up_pre).astype(jnp.bfloat16)
    result = jnp.einsum(
        "sjcf,jfd->sjcd", hidden, w_expert_down, preferred_element_type=jnp.float32
    ).astype(jnp.bfloat16)
    half_width = gate_pre.shape[-1]
    expert_out = result.reshape(experts, slot_count, model_width)
    gate_keep = gate_pre.reshape(experts, slot_count, half_width)
    up_keep = up_pre.reshape(experts, slot_count, half_width)
    returned = lax.all_to_all(expert_out, "fsdp", split_axis=0, concat_axis=0, tiled=True)
    picked_rows = (
        returned.reshape(experts * capacity, model_width)[target]
        .reshape(seq_rows, TOPK, model_width)
        .astype(jnp.float32)
    )
    ffn_part = ffn_part + jnp.sum(gate_values[:, :, None] * picked_rows, axis=1)
    ffn_sum = lax.psum_scatter(
        ffn_part.astype(jnp.bfloat16), "tp", scatter_dimension=0, tiled=True
    ).astype(jnp.float32)
    middle_own = lax.dynamic_slice_in_dim(middle, position * own_rows, own_rows, 0)
    block_out = (middle_own + ffn_sum).astype(jnp.bfloat16)
    gate_grad = lax.psum(jnp.sum(upstream[:, None, :] * picked_rows, axis=-1), "tp")
    arrived_grads = lax.all_to_all(send_grads, "fsdp", split_axis=0, concat_axis=0, tiled=True)
    half_width = gate_keep.shape[-1]
    grad_rows = arrived_grads.reshape(sources, local_experts, capacity, model_width)
    input_rows = arrived.reshape(sources, local_experts, capacity, model_width)
    gate_pre = gate_keep.reshape(sources, local_experts, capacity, half_width)
    up_pre = up_keep.reshape(sources, local_experts, capacity, half_width)
    expert_act = smooth_gate(gate_pre)
    expert_hidden = (expert_act * up_pre).astype(jnp.bfloat16)
    hidden_grad = jnp.einsum(
        "sjcd,jfd->sjcf", grad_rows, w_expert_down, preferred_element_type=jnp.float32
    )
    grad_expert_down = jnp.einsum(
        "sjcf,sjcd->jfd", expert_hidden, grad_rows, preferred_element_type=jnp.float32
    )
    gate_low = (hidden_grad * up_pre * smooth_slope(gate_pre)).astype(jnp.bfloat16)
    up_low = (hidden_grad * expert_act).astype(jnp.bfloat16)
    grad_expert_gate = jnp.einsum(
        "sjcd,sjcf->jdf", input_rows, gate_low, preferred_element_type=jnp.float32
    )
    grad_expert_up = jnp.einsum(
        "sjcd,sjcf->jdf", input_rows, up_low, preferred_element_type=jnp.float32
    )
    row_grads = jnp.einsum(
        "sjcf,jdf->sjcd", gate_low, w_expert_gate, preferred_element_type=jnp.float32
    ) + jnp.einsum("sjcf,jdf->sjcd", up_low, w_expert_up, preferred_element_type=jnp.float32)
    row_grads = row_grads.astype(jnp.bfloat16).reshape(experts, capacity, model_width)
    back_rows = lax.all_to_all(row_grads, "fsdp", split_axis=0, concat_axis=0, tiled=True)
    input_grad = jnp.sum(
        back_rows.reshape(experts * capacity, model_width)[target]
        .reshape(seq_rows, TOPK, model_width)
        .astype(jnp.float32),
        axis=1,
    )
    shared_hidden_grad = times_transposed(group_cot, full_sdown)
    grad_shared_down = transposed_times(shared_hidden, group_cot)
    sgate_low = (shared_hidden_grad * shared_up * smooth_slope(shared_gate)).astype(jnp.bfloat16)
    sup_low = (shared_hidden_grad * shared_act).astype(jnp.bfloat16)
    grad_shared_gate = transposed_times(ffn_input, sgate_low)
    grad_shared_up = transposed_times(ffn_input, sup_low)
    input_grad = (
        input_grad + times_transposed(sgate_low, full_sgate) + times_transposed(sup_low, full_sup)
    )
    input_grad = lax.psum(input_grad, "tp")
    pick_grad = gate_values * (gate_grad - jnp.sum(gate_values * gate_grad, axis=-1, keepdims=True))
    logit_low = jnp.sum(jnp.where(chosen, pick_grad[:, :, None], 0.0), axis=1).astype(jnp.bfloat16)
    grad_router = transposed_times(ffn_input, logit_low)
    input_grad = input_grad + times_transposed(logit_low, full_router)
    grad_gain_ffn = jnp.sum(input_grad * normed_two, axis=0)
    middle_grad = upstream + norm_back(input_grad, normed_two, scale_two, second_norm_gain)
    attn_grad_low = middle_grad.astype(jnp.bfloat16)
    grad_out = transposed_times(heads_out, attn_grad_low)
    heads_grad = (
        times_transposed(attn_grad_low, full_out)
        .astype(jnp.bfloat16)
        .reshape(seq_rows, kv_local, tokens_per_group, HEAD_SIZE)
    )
    again_scores = attention_scores(query_rot, rotated_key, allowed)
    attn_probs = jnp.exp(again_scores - log_total)
    probs_grad = jnp.einsum(
        "qgjd,kgd->gjqk", heads_grad, value_low, preferred_element_type=jnp.float32
    )
    value_grad = (
        jnp.einsum(
            "gjqk,qgjd->kgd",
            attn_probs.astype(jnp.bfloat16),
            heads_grad,
            preferred_element_type=jnp.float32,
        )
        .astype(jnp.bfloat16)
        .reshape(seq_rows, kv_local * HEAD_SIZE)
    )
    score_low = (
        attn_probs * (probs_grad - jnp.sum(attn_probs * probs_grad, axis=-1, keepdims=True))
    ).astype(jnp.bfloat16)
    query_grad = jnp.einsum(
        "gjqk,kgd->qgjd", score_low, rotated_key, preferred_element_type=jnp.float32
    ) * HEAD_SIZE ** (-0.5)
    key_grad = jnp.einsum(
        "gjqk,qgjd->kgd", score_low, query_rot, preferred_element_type=jnp.float32
    ) * HEAD_SIZE ** (-0.5)
    query_low = (
        apply_rotary(
            query_grad.reshape(seq_rows, heads_local, HEAD_SIZE), rotary_cosine, -rotary_sine
        )
        .astype(jnp.bfloat16)
        .reshape(seq_rows, heads_local * HEAD_SIZE)
    )
    key_low = (
        apply_rotary(key_grad, rotary_cosine, -rotary_sine)
        .astype(jnp.bfloat16)
        .reshape(seq_rows, kv_local * HEAD_SIZE)
    )
    grad_query = transposed_times(attn_input, query_low)
    grad_key = transposed_times(attn_input, key_low)
    grad_value = transposed_times(attn_input, value_grad)
    attn_in_grad = (
        times_transposed(query_low, full_query)
        + times_transposed(key_low, full_key)
        + times_transposed(value_grad, full_value)
    )
    attn_in_grad = lax.psum(attn_in_grad.astype(jnp.bfloat16), "tp").astype(jnp.float32)
    grad_gain_attn = jnp.sum(attn_in_grad * normed_one, axis=0)
    token_grad = middle_grad + norm_back(attn_in_grad, normed_one, scale_one, first_norm_gain)
    grad_tokens = lax.dynamic_slice_in_dim(token_grad, position * own_rows, own_rows, 0)
    everything = (
        lax.psum_scatter(grad_query, "fsdp", scatter_dimension=0, tiled=True),
        lax.psum_scatter(grad_key, "fsdp", scatter_dimension=0, tiled=True),
        lax.psum_scatter(grad_value, "fsdp", scatter_dimension=0, tiled=True),
        lax.psum_scatter(grad_out, "fsdp", scatter_dimension=1, tiled=True),
        lax.psum_scatter(grad_gain_attn, "fsdp", scatter_dimension=0, tiled=True),
        lax.psum_scatter(grad_shared_gate, "fsdp", scatter_dimension=0, tiled=True),
        lax.psum_scatter(grad_shared_up, "fsdp", scatter_dimension=0, tiled=True),
        lax.psum_scatter(grad_shared_down, "fsdp", scatter_dimension=1, tiled=True),
        lax.psum_scatter(grad_router, "fsdp", scatter_dimension=0, tiled=True),
        lax.psum_scatter(grad_gain_ffn, "fsdp", scatter_dimension=0, tiled=True),
    )
    attn_grads = everything[:5]
    ffn_grads = everything[5:]
    return (
        block_out,
        grad_tokens,
        attn_grads[4],
        attn_grads[0],
        attn_grads[1],
        attn_grads[2],
        attn_grads[3],
        ffn_grads[4],
        ffn_grads[3],
        ffn_grads[0],
        ffn_grads[1],
        ffn_grads[2],
        grad_expert_gate,
        grad_expert_up,
        grad_expert_down,
    )


PAIRS = ((4, 8), (0, 1), (9, 12), (14, 6), (15, 11), (13, 7), (5, 10), (2, 3))


class Flight:
    pass


class Take:
    def __init__(self, flight):
        self.flight = flight

    def __getattr__(self, name):
        return vars(self.flight).pop(name)


def hop(values, bit):
    count = lax.axis_size("fsdp")
    return lax.ppermute(values, "fsdp", [(i, i ^ bit) for i in range(count)])


def swap(values):
    return lax.ppermute(values, "tp", [(0, 1), (1, 0)])


def route(values, rule):
    pairs = []
    for group in range(lax.axis_size("fsdp")):
        for side in range(2):
            target = rule(group, side)
            if target is not None:
                pairs.append((group * 2 + side, target[0] * 2 + target[1]))
    return lax.ppermute(values, ("fsdp", "tp"), pairs)


def is_home(group, side):
    return (group // 4) % 2 == side


def home_far(group, side):
    return (group ^ 8, side) if is_home(group, side) else None


def home_near(group, side):
    return (group ^ 4, side) if is_home(group, side) else None


def near_home(group, side):
    return None if is_home(group, side) else (group ^ 4, side)


def home_side(group, side):
    return (group, 1 - side) if is_home(group, side) else None


def pack_out_a(group, side):
    return (group ^ 4, 1) if side == group // 8 else (group ^ 8, 0)


def pack_out_b(group, side):
    return (group, 0) if side == group // 8 else (group ^ 12, 1)


def pack_back_a(group, side):
    return (group ^ (8 if side == 0 else 4), group // 8)


def pack_back_b(group, side):
    return (group ^ (0 if side == 0 else 12), group // 8)


def plane_one(group, side):
    return (group ^ (1 if side == 0 else 2), side)


def plane_two(group, side):
    return (group ^ (2 if side == 0 else 1), side)


def cot_first_route(group, side):
    return (group ^ (8 if side == 0 else 4), side)


def cot_second_route(group, side):
    return (group ^ 4, 1) if side == 0 else None


COT_CARRIED = ((0, 8, 1, 9, 2, 10, 3, 11), (4, 12, 6, 14, 5, 13, 7, 15))
CARRIED = ((0, 8, 1, 9, 2, 10, 3, 11), (12, 4, 14, 6, 13, 5, 15, 7))


def join(*parts):
    return jnp.concatenate(parts, axis=0)


def plus(left, right):
    return (left.astype(jnp.float32) + right.astype(jnp.float32)).astype(jnp.bfloat16)


def piece(view):
    array, start, rows = view
    return array if array.shape[0] == rows else array[start : start + rows]


def whole_view(array):
    return (array, 0, array.shape[0])


def as_tuple(index):
    return index if isinstance(index, tuple) else (index,)


LINE = (0, 4, 8, 12)


def exchange_plane(block_for):
    parts = [jnp.stack([block_for(line + plane) for line in LINE]) for plane in range(4)]
    parts = [parts[0]] + [hop(parts[plane], plane) for plane in (1, 2, 3)]
    return {line: jnp.stack([part[i] for part in parts]) for i, line in enumerate(LINE)}


def exchange_line(sent, lines):
    return {line: hop(sent[line], line) if line else sent[line] for line in lines}


def exchange_join(got, me):
    rows, columns = got[0].shape[1:]
    whole = jnp.zeros((16, rows, columns), got[0].dtype)
    for line, blocks in got.items():
        for plane in range(4):
            whole = lax.dynamic_update_slice_in_dim(
                whole, blocks[plane : plane + 1], me ^ (line + plane), 0
            )
    return whole


def chosen_slots(place_ref, which, slots):
    numbers = lax.broadcasted_iota(jnp.int32, (slots, place_ref.shape[2]), 0)
    return numbers.astype(jnp.float32) == place_ref[0, which : which + 1, :]


def expert_kernel(first, number, starts, *refs):
    side_ref, tok_refs, cot_refs = refs[0], refs[1:5], refs[5:9]
    w_gate_ref, w_up_ref, w_down_ref, in_ref, out_ref = refs[9:14]
    refs = refs[14 if first else 21 :]
    stores = refs[:7]
    back_refs, note_ref = refs[7:10], refs[10]
    (
        toks,
        cots,
        rows,
        cot_rows,
        dys,
        hids,
        dboth,
        shareds,
        w_both,
        w_down,
        w_in,
        w_out,
        gate_terms,
        sems,
        store_sems,
    ) = refs[11:]
    part_rows = back_refs[0].shape[0]
    starts, spots = starts
    side = side_ref[0]
    seq_rows = 2 * part_rows
    hidden = w_down.shape[0]
    tile = 256
    slots = rows.shape[0] // 2

    parts = [pl.ds(i * part_rows, part_rows) for i in range(4)]
    pairs = [
        (tok_refs[i].at[pl.ds(starts[i], part_rows)], toks.at[parts[i]]) for i in range(4)
    ]
    pairs += [(in_ref, w_in)]
    pairs += [(None, cots.at[parts[i]]) for i in range(4)]
    pairs += [(out_ref, w_out)]
    for start in range(0, hidden, tile):
        cut = pl.ds(start, tile)
        pairs += [
            (w_gate_ref.at[0, :, cut], w_both.at[:, cut]),
            (w_up_ref.at[0, :, cut], w_both.at[:, pl.ds(hidden + start, tile)]),
            (w_down_ref.at[0, cut], w_down.at[cut]),
        ]
    def cot_copy(which, half, source):
        row = spots[which][0] * seq_rows + (side if half == 0 else 1 - side) * part_rows
        index = 5 + 2 * which + half
        return pltpu.make_async_copy(
            source.at[pl.ds(pl.multiple_of(row, part_rows), part_rows)],
            pairs[index][1],
            sems.at[index],
        )

    loads = []
    for index, (source, target) in enumerate(pairs):
        if source is None:
            which, half = divmod(index - 5, 2)
            mine, other = cot_refs[2 * which], cot_refs[2 * which + 1]
            is_mine = side == spots[which][1]

            @pl.when(is_mine)
            def start_mine(which=which, half=half, mine=mine):
                cot_copy(which, half, mine).start()

            @pl.when(jnp.logical_not(is_mine))
            def start_other(which=which, half=half, other=other):
                cot_copy(which, half, other).start()

            loads.append(cot_copy(which, half, mine))
        else:
            loads.append(pltpu.make_async_copy(source, target, sems.at[index]))
            loads[-1].start()

    sent = []

    def store(index, source):
        target = stores[index].at[pl.ds(number * source.shape[0], source.shape[0])]
        copy = pltpu.make_async_copy(source, target, store_sems.at[index])
        copy.start()
        sent.append(copy)

    gate_loads = []
    experts, term_width = gate_terms.shape[0] // 4, gate_terms.shape[1]
    for i in range(4):
        source = tok_refs[i].at[pl.ds(starts[i] + part_rows, experts), pl.ds(0, term_width)]
        target = gate_terms.at[pl.ds(i * experts, experts)]
        gate_loads.append(pltpu.make_async_copy(source, target, store_sems.at[7 + i]))
        gate_loads[-1].start()
    for load in gate_loads:
        load.wait()
    expert = side_ref[1]
    numbers = lax.broadcasted_iota(jnp.int32, (experts, term_width), 0)
    before = lax.broadcasted_iota(jnp.int32, (seq_rows, seq_rows), 0) < (
        lax.broadcasted_iota(jnp.int32, (seq_rows, seq_rows), 1)
    )
    before = before.astype(jnp.float32).astype(jnp.bfloat16)
    for which in range(2):
        halves = []
        for i in (2 * which, 2 * which + 1):
            terms = gate_terms[i * experts : (i + 1) * experts, :].astype(jnp.float32)
            row = jnp.sum(jnp.where(numbers == expert, terms, 0.0), axis=0, keepdims=True)
            halves.append(
                row[:, :part_rows]
                + row[:, part_rows : 2 * part_rows]
                + row[:, 2 * part_rows : 3 * part_rows]
            )
        gate_row = jnp.concatenate(halves, axis=1)
        flags = jnp.where(gate_row >= 0.0, 1.0, 0.0)
        ranks = product(
            jnp.broadcast_to(flags, (8, seq_rows)).astype(jnp.bfloat16), before
        )[:1]
        note_ref[2 + which : 3 + which, :] = jnp.where(flags > 0.0, ranks, -1.0)
        note_ref[4 + which : 5 + which, :] = gate_row
    for load in loads[:4]:
        load.wait()
    slot_numbers = lax.broadcasted_iota(jnp.int32, (slots, seq_rows), 0).astype(jnp.float32)
    chosen = [slot_numbers == note_ref[2 + which : 3 + which, :] for which in range(2)]
    low = [c.astype(jnp.bfloat16) for c in chosen]
    for which in range(2):
        span = slice(which * slots, (which + 1) * slots)
        seq = slice(which * seq_rows, (which + 1) * seq_rows)
        rows[span, :] = product(low[which], toks[seq, :]).astype(jnp.bfloat16)
    store(0, rows)
    store(5, toks)
    loads[4].wait()
    shared_pre = product(toks[...], w_in[...])
    for load in loads[5:9]:
        load.wait()
    gates = [
        jnp.sum(
            jnp.where(chosen[which], note_ref[4 + which : 5 + which, :], 0.0),
            axis=1,
            keepdims=True,
        )
        for which in range(2)
    ]
    for which in range(2):
        span = slice(which * slots, (which + 1) * slots)
        seq = slice(which * seq_rows, (which + 1) * seq_rows)
        picked = product(low[which], cots[seq, :])
        cot_rows[span, :] = picked.astype(jnp.bfloat16)
        dys[span, :] = (gates[which] * picked).astype(jnp.bfloat16)
    store(1, dys)
    store(6, cots)
    gates = jnp.concatenate(gates, axis=0)
    loads[9].wait()
    half = w_out.shape[0]
    pre, up = shared_pre[:, :half], shared_pre[:, half:]
    hid_grad = times_transposed(cots[...], w_out[...])
    sigmoid = 1.0 / (1.0 + jnp.exp(-pre))
    act = pre * sigmoid
    shareds[:, :half] = (hid_grad * up * (sigmoid * (1.0 + pre * (1.0 - sigmoid)))).astype(
        jnp.bfloat16
    )
    shareds[:, half : 2 * half] = (hid_grad * act).astype(jnp.bfloat16)
    shareds[:, 2 * half :] = (act * up).astype(jnp.bfloat16)
    store(4, shareds)

    picks = jnp.zeros_like(gates)
    for index, start in enumerate(range(0, hidden, tile)):
        for load in loads[10 + 3 * index : 13 + 3 * index]:
            load.wait()
        cut = slice(start, start + tile)
        cut_up = slice(hidden + start, hidden + start + tile)
        gate_pre = product(rows[...], w_both[:, cut])
        up_pre = product(rows[...], w_both[:, cut_up])
        cot_hidden = times_transposed(cot_rows[...], w_down[cut, :])
        sigmoid = 1.0 / (1.0 + jnp.exp(-gate_pre))
        act = gate_pre * sigmoid
        hid = (act * up_pre).astype(jnp.bfloat16)
        grad = gates * cot_hidden
        hids[:, cut] = hid
        dboth[:, cut] = (grad * up_pre * (sigmoid * (1.0 + gate_pre * (1.0 - sigmoid)))).astype(
            jnp.bfloat16
        )
        dboth[:, cut_up] = (grad * act).astype(jnp.bfloat16)
        picks = picks + jnp.sum(hid.astype(jnp.float32) * cot_hidden, axis=1, keepdims=True)
    store(2, hids)
    store(3, dboth)
    back_rows = times_transposed(dboth[...], w_both[...]).astype(jnp.bfloat16)
    for which in range(2):
        span = slice(which * slots, (which + 1) * slots)
        seq = slice(which * seq_rows, (which + 1) * seq_rows)
        back = transposed_times(low[which], back_rows[span, :]) + times_transposed(
            shareds[seq, : 2 * half], w_in[...]
        )
        back_refs[which][...] = back[:part_rows, :].astype(jnp.bfloat16)
        back_refs[2][which * part_rows : (which + 1) * part_rows, :] = back[
            part_rows:, :
        ].astype(jnp.bfloat16)
        note_ref[which : which + 1, :] = jnp.sum(
            jnp.where(chosen[which], picks[span, :], 0.0), axis=0, keepdims=True
        )
    for copy in sent:
        copy.wait()


def expert_call(number, position, tokens, cots, weights, kept):
    w_gate, w_up, w_down, shared_in, shared_out = weights
    experts, width = 16, tokens[0][0].shape[1]
    part_rows = tokens[0][2] - experts
    starts = (tuple(view[1] for view in tokens), tuple(cot[2:] for cot in cots))
    slots = part_rows
    hidden = w_gate.shape[2]
    calls = len(PAIRS)
    first = kept is None
    low = jnp.bfloat16
    some = pl.BlockSpec(memory_space=pl.ANY)
    backs = [pl.BlockSpec((n * part_rows, width), lambda i: (0, 0)) for n in (1, 1, 2)]
    note = pl.BlockSpec((6, 2 * part_rows), lambda i: (0, 0))
    in_specs = [pl.BlockSpec(memory_space=pltpu.SMEM)] + [some] * 13
    operands = [position, *(view[0] for view in tokens)]
    operands += [array for cot in cots for array in cot[:2]]
    operands += weights
    aliases = {}
    if not first:
        aliases = {len(operands) + i: i for i in range(7)}
        in_specs += [some] * 7
        operands += list(kept)
    shared_width = 3 * shared_out.shape[0]
    kept_shapes = [(2 * slots, width)] * 2 + [(2 * slots, hidden), (2 * slots, 2 * hidden)]
    kept_shapes += [(4 * part_rows, c) for c in (shared_width, width, width)]
    out_shape = [jax.ShapeDtypeStruct((calls * r, c), low) for r, c in kept_shapes]
    out_shape += [jax.ShapeDtypeStruct((n * part_rows, width), low) for n in (1, 1, 2)]
    out_shape += [jax.ShapeDtypeStruct((6, 2 * part_rows), jnp.float32)]
    results = pl.pallas_call(
        lambda *refs: expert_kernel(first, number, starts, *refs),
        grid=(1,),
        in_specs=in_specs,
        out_specs=[some] * 7 + backs + [note],
        out_shape=out_shape,
        scratch_shapes=[
            pltpu.VMEM((4 * part_rows, width), low),
            pltpu.VMEM((4 * part_rows, width), low),
            pltpu.VMEM((2 * slots, width), low),
            pltpu.VMEM((2 * slots, width), low),
            pltpu.VMEM((2 * slots, width), low),
            pltpu.VMEM((2 * slots, hidden), low),
            pltpu.VMEM((2 * slots, 2 * hidden), low),
            pltpu.VMEM((4 * part_rows, shared_width), low),
            pltpu.VMEM((width, 2 * hidden), low),
            pltpu.VMEM((hidden, width), low),
            pltpu.VMEM(shared_in.shape, low),
            pltpu.VMEM(shared_out.shape, low),
            pltpu.VMEM((4 * experts, 3 * part_rows), low),
            pltpu.SemaphoreType.DMA((10 + 3 * (hidden // 256),)),
            pltpu.SemaphoreType.DMA((11,)),
        ],
        input_output_aliases=aliases,
        compiler_params=pltpu.CompilerParams(vmem_limit_bytes=36 * 1024 * 1024),
        cost_estimate=pl.CostEstimate(
            flops=4 * slots * width * (5 * hidden + 10 * slots),
            bytes_accessed=24 * 1024 * 1024,
            transcendentals=slots * hidden,
        ),
        name="expert_pass",
    )(*operands)
    return results[:7], results[7:10], results[10]


def output_kernel(
    place_ref, gate_ref, hid_ref, shared_ref, w_down_ref, w_out_ref, own_ref, other_ref
):
    part_rows = own_ref.shape[0] // 2
    seq_rows = 2 * part_rows
    slots = hid_ref.shape[0] // 2
    half = w_out_ref.shape[0]
    result = product(hid_ref[...], w_down_ref[0])
    for which in range(2):
        chosen = chosen_slots(place_ref, which, slots)
        gates = jnp.sum(
            jnp.where(chosen, gate_ref[0, which : which + 1, :], 0.0), axis=1, keepdims=True
        )
        gated = (gates * result[which * slots : (which + 1) * slots, :]).astype(jnp.bfloat16)
        seq = slice(which * seq_rows, (which + 1) * seq_rows)
        out = transposed_times(chosen.astype(jnp.bfloat16), gated) + product(
            shared_ref[seq, 2 * half :], w_out_ref[...]
        )
        rows = slice(which * part_rows, (which + 1) * part_rows)
        own_ref[rows, :] = out[:part_rows, :].astype(jnp.bfloat16)
        other_ref[rows, :] = out[part_rows:, :].astype(jnp.bfloat16)


def output_call(places, gates, hids, shareds, w_down, shared_out):
    calls = len(PAIRS)
    slots, hidden = places.shape[2] // 2, hids.shape[1]
    width = shared_out.shape[1]
    tok_rows = shareds.shape[0] // calls
    row = pl.BlockSpec((1, 2, places.shape[2]), lambda i: (i, 0, 0))
    half = jax.ShapeDtypeStruct((calls * tok_rows // 2, width), jnp.bfloat16)
    return pl.pallas_call(
        output_kernel,
        grid=(calls,),
        in_specs=[
            row,
            row,
            pl.BlockSpec((2 * slots, hidden), lambda i: (i, 0)),
            pl.BlockSpec((tok_rows, shareds.shape[1]), lambda i: (i, 0)),
            pl.BlockSpec(w_down.shape, lambda i: (0, 0, 0)),
            pl.BlockSpec(shared_out.shape, lambda i: (0, 0)),
        ],
        out_specs=[pl.BlockSpec((tok_rows // 2, width), lambda i: (i, 0))] * 2,
        out_shape=[half] * 2,
        compiler_params=pltpu.CompilerParams(vmem_limit_bytes=48 * 1024 * 1024),
        cost_estimate=pl.CostEstimate(
            flops=4 * slots * width * (hidden + 4 * slots) * calls,
            bytes_accessed=32 * 1024 * 1024,
            transcendentals=0,
        ),
        name="expert_outputs",
    )(places, gates, hids, shareds, w_down, shared_out)


def gathered_shards(
    tokens_in,
    cotangent,
    doc_ids,
    routes,
    gain_attn,
    w_query,
    w_key,
    w_value,
    w_out,
    gain_ffn,
    w_router,
    w_shared_gate,
    w_shared_up,
    w_shared_down,
    w_expert_gate,
    w_expert_up,
    w_expert_down,
):
    low = jnp.bfloat16
    own_rows, width = tokens_in.shape
    seq_rows = doc_ids.shape[0]
    experts = w_router.shape[1]
    sources = lax.axis_size("fsdp")
    capacity = max(2, 4 * seq_rows * TOPK // (3 * experts))
    me = lax.axis_index("fsdp")
    side = lax.axis_index("tp")
    relative = jnp.arange(sources, dtype=jnp.int32) ^ me
    query_width, kv_width = w_query.shape[1], w_key.shape[1]
    heads_local, kv_local = query_width // HEAD_SIZE, kv_width // HEAD_SIZE
    per_kv = QUERY_HEADS // KEY_VALUE_HEADS

    state = Flight()
    take = Take(state)
    state.expert_grads = {}

    def barrier():
        vars(state).update(lax.optimization_barrier(dict(vars(state))))

    def launch(moves):
        got = []
        for name, parts in moves.items():
            for starts, ends in parts:
                starts, ends = as_tuple(starts), as_tuple(ends)
                blocks = [vars(state)[name][index] for index in starts]
                value = blocks[0] if len(blocks) == 1 else join(*blocks)
                got.append((name, ends, hop(value, starts[0] ^ ends[0])))
        return got

    def meet(got, value):
        blocks, value = lax.optimization_barrier(([block for *_, block in got], value))
        return [(*key, block) for (*key, _), block in zip(got, blocks, strict=True)], value

    def settle(got):
        for name, ends, value in got:
            rows = value.shape[0] // len(ends)
            for place, end in enumerate(ends):
                part = piece((value, place * rows, rows))
                if name not in summed:
                    vars(state)[name][end] = part
                    views[end] = (value, place * rows, rows)
                elif end in vars(state)[name]:
                    vars(state)[name][end] = plus(vars(state)[name][end], part)
                else:
                    later[name, end] = part

    def stage(moves, work=None):
        barrier()
        if work is not None:
            work()
        settle(launch(moves))

    summed = ("back", "out")
    later = {}
    views = {}

    small = jnp.concatenate([gain_attn[:, None], gain_ffn[:, None], w_router], axis=1)
    small_width = small.shape[1]
    small = jnp.pad(small, ((0, 0), (0, -small_width % 128)))
    position = jnp.stack([side, me]).astype(jnp.int32)

    layer = me // 4
    here = side == layer // 2
    home = layer % 2 == side
    parity_b = jnp.where(here, layer, layer ^ 3) % 2
    group_width = per_kv * HEAD_SIZE
    pack_width = 2 * group_width + 2 * HEAD_SIZE
    qkv_width = group_width + 2 * HEAD_SIZE
    out_t = w_out.T
    packs = [
        jnp.concatenate(
            [
                w_query[:, j * group_width : (j + 1) * group_width],
                w_key[:, j * HEAD_SIZE : (j + 1) * HEAD_SIZE],
                w_value[:, j * HEAD_SIZE : (j + 1) * HEAD_SIZE],
                out_t[:, j * group_width : (j + 1) * group_width],
                small,
            ],
            axis=1,
        )
        for j in range(kv_local)
    ]
    state.packs = tuple(
        jnp.where(parity_b == parity, packs[0], packs[1]) for parity in (1, 0)
    )
    state.tokens = tokens_in
    state.cot = cotangent

    def whole_of(own):
        other = swap(own)
        return jnp.where(side == 0, join(own, other), join(other, own))

    def carried(number, mine):
        zero, one = CARRIED[0][number], CARRIED[1][number]
        return me ^ (jnp.where(side == 0, zero, one) if mine else jnp.where(side == 0, one, zero))

    slice_width = w_shared_gate.shape[1] // sources
    pad_width = -slice_width % 128
    wide = slice_width + pad_width
    state.shared_parts = (w_shared_gate, w_shared_up, w_shared_down)

    def shard_for(index):
        return lax.dynamic_index_in_dim(shards_in, me ^ index, 0, keepdims=False)

    doc_rows = jnp.zeros((16, width), low).at[0, :seq_rows].set(doc_ids.astype(low))
    barrier()
    pack_a, pack_b = (
        route(pack, rule)
        for pack, rule in zip(take.packs, (pack_out_a, pack_out_b), strict=True)
    )
    state.base = join(pack_b, pack_a)
    state.tokens = join(whole_of(take.tokens), doc_rows)
    state.cot = whole_of(take.cot)
    barrier()
    base, whole_tokens = take.base, state.tokens
    state.early = join(base, route(base, plane_one))
    state.far = route(whole_tokens, home_far)
    state.near = route(whole_tokens, home_near)
    shared_parts = take.shared_parts
    shards_in = jnp.concatenate(
        [
            jnp.pad(
                part.reshape(part.shape[0], sources, slice_width),
                ((0, 0), (0, 0), (0, pad_width)),
            )
            for part in (*shared_parts[:2], shared_parts[2].T)
        ],
        axis=2,
    ).transpose(1, 0, 2)

    state.shards = exchange_plane(shard_for)
    barrier()
    early, far = state.early, state.far
    state.second = route(early, plane_two)
    state.early_other = swap(early)
    state.cross = route(far, home_near)
    state.shards_got = exchange_line(state.shards, (0, 12))
    barrier()
    second, early, early_other = take.second, take.early, take.early_other
    line_parts = [
        jnp.where(home, one, two)
        for one, two in ((take.tokens, take.near), (take.far, take.cross))
    ]
    token_rows = join(*(part[:seq_rows] for part in line_parts))
    docs = jnp.stack([part[seq_rows, :seq_rows] for part in line_parts])
    state.cot_one = route(state.cot, cot_first_route)
    state.shards_got.update(exchange_line(state.shards, (8,)))
    pack_rows = pack_a.shape[0]
    full_weights = jnp.zeros((width, pack_a.shape[1]), low)
    number = 0
    for part, got in ((early, early_other), (second, swap(second))):
        for place in range(part.shape[0] // pack_rows):
            rows = slice(place * pack_rows, (place + 1) * pack_rows)
            for block, mine in ((part[rows], True), (got[rows], False)):
                full_weights = lax.dynamic_update_slice_in_dim(
                    full_weights, block, carried(number, mine) * pack_rows, 0
                )
                full_weights = with_layout_constraint(
                    full_weights, Layout(major_to_minor=(0, 1))
                )
            number += 1

    rotary_cosine, rotary_sine = (
        jnp.tile(table, (2, 1)) for table in rotary_tables(seq_rows)
    )
    order_ids = jnp.arange(seq_rows)
    allowed = (docs[:, :, None] == docs[:, None, :]) & (
        order_ids[:, None] >= order_ids[None, :]
    )
    small_all = full_weights[:, pack_width:]
    gain_one = small_all[:, 0].astype(jnp.float32)
    gain_two = small_all[:, 1].astype(jnp.float32)
    full_router = small_all[:, 2:small_width]
    scale = HEAD_SIZE ** (-0.5)

    def attend():
        rows = token_rows.astype(jnp.float32)
        attn_input = (rows * rms_scale(rows) * gain_one).astype(low)
        state.attn_input = attn_input
        projected = product(attn_input, full_weights[:, :qkv_width])
        query_rot = apply_rotary(
            projected[:, :group_width].reshape(2 * seq_rows, per_kv, HEAD_SIZE),
            rotary_cosine,
            rotary_sine,
        )
        query_rot = query_rot.astype(low).reshape(2, seq_rows, per_kv, HEAD_SIZE)
        rotated_key = apply_rotary(
            projected[:, group_width : group_width + HEAD_SIZE][:, None, :],
            rotary_cosine,
            rotary_sine,
        )
        rotated_key = rotated_key.astype(low).reshape(2, seq_rows, HEAD_SIZE)
        value_low = projected[:, group_width + HEAD_SIZE :].astype(low)
        value_low = value_low.reshape(2, seq_rows, HEAD_SIZE)
        scores = (
            jnp.einsum("sqjd,skd->sjqk", query_rot, rotated_key, preferred_element_type=jnp.float32)
            * scale
        )
        scores = jnp.where(allowed[:, None], scores, -1e30)
        top_score = jnp.max(scores, axis=-1, keepdims=True)
        weights = jnp.exp(scores - top_score)
        attn_probs = weights / jnp.sum(weights, axis=-1, keepdims=True)
        probs_low = attn_probs.astype(low)
        heads_out = (
            jnp.einsum("sjqk,skd->sqjd", probs_low, value_low, preferred_element_type=jnp.float32)
            .astype(low)
            .reshape(2 * seq_rows, group_width)
        )
        state.attention = (query_rot, rotated_key, value_low, attn_probs, probs_low)
        state.heads_out = heads_out
        state.branch = times_transposed(heads_out, full_weights[:, qkv_width:pack_width]).astype(low)

    attend()
    barrier()

    own_routes = lax.dynamic_slice_in_dim(routes, side * own_rows, own_rows, 0)
    routed = jnp.any(
        own_routes[:, :, None] == jnp.arange(experts, dtype=jnp.int32)[None, None, :], axis=1
    )

    def near_sum(partial):
        own_part, far_part = partial[:seq_rows], partial[seq_rows:]
        state.far_part = plus(far_part, route(far_part, near_home))
        state.own_part = own_part.astype(jnp.float32) + route(own_part, near_home).astype(
            jnp.float32
        )

    def far_sum():
        return take.own_part + route(take.far_part, home_far).astype(jnp.float32)

    def own_of(own_sum):
        mine = lax.dynamic_slice_in_dim(own_sum, side * own_rows, own_rows, 0)
        other = lax.dynamic_slice_in_dim(own_sum, (1 - side) * own_rows, own_rows, 0)
        return jnp.where(home, mine, route(other, home_side))

    near_sum(take.branch)
    cot_whole, cot_one = take.cot, take.cot_one
    cot_two = route(cot_one, cot_second_route)
    state.cot_base = jnp.where(side == 0, join(cot_whole, cot_one), join(cot_one, cot_two))
    barrier()
    cot_base = take.cot_base
    state.cot_first = route(cot_base, plane_one)
    cot_base_other = swap(cot_base)
    state.shards_got.update(exchange_line(take.shards, (4,)))
    state.own_sum = far_sum()
    state.cot_base_other = cot_base_other
    barrier()
    own_sum, cot_base_other = take.own_sum, take.cot_base_other
    middle = tokens_in.astype(jnp.float32) + own_of(own_sum)
    state.middle = middle
    state.scale_two = scale_two = rms_scale(middle)
    normed_two = middle * scale_two
    state.normed_two = normed_two
    state.ffn = {0: (normed_two * gain_two).astype(low)}

    def cot_view(index):
        for core, order in enumerate(COT_CARRIED):
            if index in order:
                part, place = divmod(order.index(index), 2)
                if part == 3:
                    part, place = part + place, 0
                return (*cot_parts[part], place, core)

    logits = product(state.ffn[0], full_router)
    top_pick = jnp.max(jnp.where(routed, logits, -jnp.inf), axis=-1, keepdims=True)
    gate_exp = jnp.where(routed, jnp.exp(logits - top_pick), 0.0)
    gate_values = gate_exp / jnp.sum(gate_exp, axis=-1, keepdims=True)
    state.gate_values = gate_values
    rest = jnp.where(routed, gate_values, -1.0).T
    terms = []
    for _ in range(3):
        terms.append(rest.astype(low))
        rest = rest - terms[-1].astype(jnp.float32)
    gate_rows = jnp.concatenate(terms, axis=1)
    gate_rows = jnp.pad(gate_rows, ((0, 0), (0, width - gate_rows.shape[1])))
    ffn_own = state.ffn[0]
    state.ffn[0] = join(ffn_own, gate_rows)
    block_rows = own_rows + experts

    views[0] = whole_view(state.ffn[0])
    other_views = {}
    swapping = []

    def swap_tokens(indices):
        blocks = [state.ffn[index] for index in indices]
        others = swap(blocks[0] if len(blocks) == 1 else join(*blocks))
        for place, index in enumerate(indices):
            swapping.append((index, (others, place * block_rows, block_rows)))

    def swapped():
        other_views.update(dict(swapping))
        swapping.clear()

    barrier()
    cot_first = take.cot_first
    cot_parts = {0: (cot_base, cot_base_other)}
    cot_third = route(cot_base, plane_two)
    state.cot_third = cot_third
    got = launch(dict(ffn=((0, 8), (0, 4), (0, 1), (0, 2))))
    settle(got)
    swapped()
    shared_all = exchange_join(take.shards_got, me).reshape(width, 3 * wide)
    state.shared_in = shared_all[:, : 2 * wide]
    state.shared_out = shared_all[:, 2 * wide :].T

    state.back, state.back_own, state.back_other, state.notes = {}, {}, {}, {}
    kept = None

    def experts_of(*numbers):
        def work():
            nonlocal kept
            for number in numbers:
                one, two = PAIRS[number]
                kept, back, state.notes[number] = expert_call(
                    number,
                    position,
                    (views[one], other_views[one], views[two], other_views[two]),
                    (cot_view(one), cot_view(two)),
                    (
                        w_expert_gate,
                        w_expert_up,
                        w_expert_down,
                        state.shared_in,
                        state.shared_out,
                    ),
                    kept,
                )
                state.back_own[one], state.back_own[two] = back[:2]
                state.back_other[one, two] = back[2]

        return work

    def swap_back():
        ((indices, both_rows),) = state.back_other.items()
        state.back_other.clear()
        others = swap(both_rows)
        return [
            (index, others[place * own_rows : (place + 1) * own_rows])
            for place, index in enumerate(indices)
        ]

    def merge_back(fresh):
        for index, other in fresh:
            total = plus(state.back_own.pop(index), other)
            if ("back", index) in later:
                total = plus(total, later.pop(("back", index)))
            state.back[index] = total

    def both(*works):
        def work():
            for one in works:
                one()

        return work

    plan = (
        ((4, 8, 0, 1), dict(ffn=((8, 12), (8, 9), (8, 10)))),
        ((9, 12, 2), dict(ffn=((12, 14), (2, 6), (12, 13)))),
        ((14, 6, 10), dict(ffn=((13, 15), (1, 5), (10, 11)))),
        ((13, 15, 11), dict(ffn=((2, 3), (5, 7)))),
        ((5, 3, 7), dict(back=((9, 8),))),
        ((), dict(back=((14, 12), (6, 2)))),
        ((), dict(back=((15, 13), (11, 10)))),
        ((), dict(back=((13, 12), (7, 3)))),
    )
    fresh = []
    for number, (arrived, moves) in enumerate(plan):
        barrier()
        if number in (1, 2):
            cot_last = take.cot_last
        if state.back_other:
            fresh = swap_back()
        if arrived:
            swap_tokens(arrived)
        if number == 0:
            swapped()
            cot_parts[1] = (cot_first, swap(cot_first))
        if number == 1:
            cot_third = take.cot_third
            cot_parts[2] = (cot_third, swap(cot_third))
        if number in (0, 1):
            state.cot_last = route(
                cot_first[number * seq_rows : (number + 1) * seq_rows], plane_two
            )
        if number in (1, 2):
            cot_parts[number + 2] = (cot_last, swap(cot_last))
        experts_of(number)()
        got, state.notes[number] = meet(launch(moves), state.notes[number])
        settle(got)
        swapped()
        merge_back(fresh)
        fresh = []
    barrier()
    fresh = swap_back()
    merge_back(fresh)
    del state.ffn
    state.kept = kept

    def outputs():
        hids, shareds = state.kept[2], state.kept[4]
        notes = jnp.stack([state.notes[number] for number in range(len(PAIRS))])
        state.out_own, state.out_other = output_call(
            notes[:, 2:4],
            notes[:, 4:],
            hids,
            shareds,
            w_expert_down,
            state.shared_out,
        )

    def return_picks():
        picks = jnp.concatenate([state.notes[number][:2] for number in range(len(PAIRS))], axis=0)
        picks = picks[:, :own_rows] + swap(picks[:, own_rows:])
        picks = picks[jnp.argsort(jnp.asarray(PAIRS).reshape(-1))]
        state.gate_grad = lax.all_to_all(
            picks[relative], "fsdp", split_axis=0, concat_axis=0, tiled=True
        ).T

    def expert_grads(which):
        def work():
            slot_rows, slot_dy, hids, dboth = state.kept[:4]
            hidden = hids.shape[1]
            left, right = (
                (hids, slot_dy),
                (slot_rows, dboth[:, :hidden]),
                (slot_rows, dboth[:, hidden:]),
            )[which]
            state.expert_grads[which] = transposed_times(left, right)[None]

        return work

    def shared_grads():
        shareds, all_rows, all_cots = state.kept[4:]
        both_grads = jnp.concatenate(
            [
                transposed_times(all_rows, shareds[:, : 2 * wide]),
                transposed_times(all_cots, shareds[:, 2 * wide :]),
            ],
            axis=1,
        )
        state.shared_grads = both_grads.astype(low).reshape(
            sources, width // sources, 3 * wide
        )

    def shared_grad_for(index):
        return lax.dynamic_index_in_dim(state.shared_grads, me ^ index, 0, keepdims=False)

    outputs()
    got, state.out_own = meet(
        launch(dict(back=((10, 8), ((5, 12), (1, 8))))), state.out_own
    )
    settle(got)
    barrier()
    return_picks()
    shared_grads()
    got, state.shared_grads = meet(
        launch(dict(back=((8, 0), ((3, 1), (2, 0))))), state.shared_grads
    )
    settle(got)
    out_own_rows, out_other_rows = take.out_own, swap(take.out_other)
    state.out_other_rows = out_other_rows
    barrier()
    settle(launch(dict(back=((4, 0), (2, 0)))))
    state.shards = exchange_plane(shared_grad_for)
    out_other_rows = take.out_other_rows
    state.out = {}
    for number, index in enumerate(index for pair in PAIRS for index in pair):
        rows = slice(number * own_rows, (number + 1) * own_rows)
        state.out[index] = plus(out_own_rows[rows], out_other_rows[rows])
    def middle_back():
        gate_values, gate_grad = state.gate_values, state.gate_grad
        normed_two, ffn_input = state.normed_two, ffn_own
        pick_grad = gate_values * (
            gate_grad - jnp.sum(gate_values * gate_grad, axis=-1, keepdims=True)
        )
        logit_low = jnp.where(routed, pick_grad, 0.0).astype(low)
        input_grad = state.back.pop(0).astype(jnp.float32)
        grad_router = transposed_times(ffn_input, logit_low)
        input_grad = input_grad + times_transposed(logit_low, full_router)
        grad_gain_ffn = jnp.sum(input_grad * normed_two, axis=0)
        middle_grad = cotangent.astype(jnp.float32) + norm_back(
            input_grad, normed_two, state.scale_two, gain_two
        )
        state.middle_grad = middle_grad
        state.small_two = jnp.concatenate([grad_gain_ffn[:, None], grad_router], axis=1)
        state.attn_grad = middle_grad.astype(low)

    def attention_back():
        attn_grad_low = take.attn_grad
        full_qkv, full_out = full_weights[:, :qkv_width], full_weights[:, qkv_width:pack_width]
        query_rot, rotated_key, value_low, attn_probs, probs_low = state.attention
        heads_grad = (
            product(attn_grad_low, full_out).astype(low).reshape(2, seq_rows, per_kv, HEAD_SIZE)
        )
        probs_grad = jnp.einsum(
            "sqjd,skd->sjqk", heads_grad, value_low, preferred_element_type=jnp.float32
        )
        value_grad = (
            jnp.einsum("sjqk,sqjd->skd", probs_low, heads_grad, preferred_element_type=jnp.float32)
            .astype(low)
            .reshape(2 * seq_rows, HEAD_SIZE)
        )
        score_low = (
            attn_probs * (probs_grad - jnp.sum(attn_probs * probs_grad, axis=-1, keepdims=True))
        ).astype(low)
        query_grad = (
            jnp.einsum("sjqk,skd->sqjd", score_low, rotated_key, preferred_element_type=jnp.float32)
            * scale
        )
        key_grad = (
            jnp.einsum("sjqk,sqjd->skd", score_low, query_rot, preferred_element_type=jnp.float32)
            * scale
        )
        query_low = apply_rotary(
            query_grad.reshape(2 * seq_rows, per_kv, HEAD_SIZE), rotary_cosine, -rotary_sine
        )
        key_low = apply_rotary(
            key_grad.reshape(2 * seq_rows, 1, HEAD_SIZE), rotary_cosine, -rotary_sine
        )
        qkv_low = jnp.concatenate(
            [
                query_low.astype(low).reshape(2 * seq_rows, group_width),
                key_low.astype(low).reshape(2 * seq_rows, HEAD_SIZE),
                value_grad,
            ],
            axis=1,
        )
        attn_in_grad = times_transposed(qkv_low, full_qkv)
        state.attn_in_grad = attn_in_grad.astype(low)
        rows = token_rows.astype(jnp.float32)
        grad_gain_attn = jnp.sum(attn_in_grad * (rows * rms_scale(rows)), axis=0)
        small_grads = jnp.concatenate([grad_gain_attn[:, None], take.small_two], axis=1)
        grads = jnp.concatenate(
            [
                transposed_times(state.attn_input, qkv_low).astype(low),
                transposed_times(attn_grad_low, state.heads_out).astype(low),
                jnp.pad(small_grads.astype(low), ((0, 0), (0, -small_width % 128))),
            ],
            axis=1,
        )
        state.grads = with_layout_constraint(grads, Layout(major_to_minor=(0, 1)))

    def split_grads():
        grads = take.grads
        return tuple(
            join(
                *(
                    lax.dynamic_slice_in_dim(grads, carried(n, mine) * pack_rows, pack_rows, 0)
                    for n in range(len(CARRIED[0]))
                )
            )
            for mine in (True, False)
        )

    barrier()
    middle_back()
    state.whole = whole_of(take.attn_grad)
    barrier()
    whole_grad = state.whole
    state.far = route(whole_grad, home_far)
    state.near = route(whole_grad, home_near)
    expert_grads(0)()
    got, state.expert_grads[0] = meet(
        launch(dict(out=(((3, 1), (2, 0)), ((15, 14), (13, 12))))), state.expert_grads[0]
    )
    settle(got)
    barrier()
    state.cross = route(state.far, home_near)
    expert_grads(1)()
    got, state.expert_grads[1] = meet(
        launch(dict(out=(((11, 13), (10, 12)), ((7, 2), (5, 0))))), state.expert_grads[1]
    )
    settle(got)
    state.shards_got = exchange_line(state.shards, (0, 4, 12))
    barrier()
    state.attn_grad = jnp.where(
        home,
        join(take.whole, take.far),
        join(take.near, take.cross),
    )
    attention_back()
    barrier()
    kept_part, sent_part = split_grads()
    state.total = plus(kept_part, swap(sent_part))
    near_sum(take.attn_in_grad)
    state.shards_got.update(exchange_line(take.shards, (8,)))
    settle(launch(dict(out=(((9, 5), (8, 4)), ((10, 6), (8, 4))))))
    expert_grads(2)()
    barrier()
    rows = state.total.shape[0] // 2
    state.total = plus(state.total[:rows], route(state.total[rows:], plane_two))
    state.own_sum = far_sum()
    settle(launch(dict(out=((12, 8),))))
    barrier()
    settle(launch(dict(out=((8, 0), (4, 0)))))
    shared_back = exchange_join(take.shards_got, me)
    shared_back = shared_back.transpose(1, 0, 2).astype(jnp.float32)
    state.shared_sums = [
        shared_back[:, :, i * wide : i * wide + slice_width].reshape(width // sources, -1)
        for i in range(3)
    ]
    rows = state.total.shape[0] // 2
    state.total = plus(state.total[:rows], route(state.total[rows:], plane_one))
    attn_in_grad = own_of(take.own_sum)
    tokens_float = tokens_in.astype(jnp.float32)
    scale_one = rms_scale(tokens_float)
    normed_own = tokens_float * scale_one
    state.grad_tokens = take.middle_grad + norm_back(
        attn_in_grad, normed_own, scale_one, gain_one
    )
    barrier()
    part_b = route(state.total[:pack_rows], pack_back_b).astype(jnp.float32)
    part_a = route(state.total[pack_rows:], pack_back_a).astype(jnp.float32)
    packs_back = (
        jnp.where(parity_b == 0, part_b, part_a),
        jnp.where(parity_b == 0, part_a, part_b),
    )

    grad_shared_gate, grad_shared_up, grad_shared_down = state.shared_sums
    small_sum = sum(part[:, pack_width : pack_width + small_width] for part in packs_back)
    small_sum = small_sum + swap(small_sum)
    block_out = (state.middle + state.out[0].astype(jnp.float32)).astype(low)
    cuts = (0, group_width, group_width + HEAD_SIZE, qkv_width, pack_width)
    grad_query, grad_key, grad_value, grad_out_t = (
        jnp.concatenate([part[:, start:stop] for part in packs_back], axis=1)
        for start, stop in zip(cuts[:-1], cuts[1:], strict=True)
    )
    return (
        block_out,
        state.grad_tokens,
        small_sum[:, 0],
        grad_query,
        grad_key,
        grad_value,
        grad_out_t.T,
        small_sum[:, 1],
        small_sum[:, 2:],
        grad_shared_gate,
        grad_shared_up,
        grad_shared_down.T,
        state.expert_grads[1],
        state.expert_grads[2],
        state.expert_grads[0],
    )


def solution(mesh):
    wide = mesh.shape["fsdp"] == 16 and mesh.shape["tp"] == 2
    return jax.shard_map(
        gathered_shards if wide else shards,
        mesh=mesh,
        in_specs=(
            P(("fsdp", "tp"), None),
            P(("fsdp", "tp"), None),
            P("fsdp"),
            P("fsdp", None),
            P("fsdp"),
            P("fsdp", "tp"),
            P("fsdp", "tp"),
            P("fsdp", "tp"),
            P("tp", "fsdp"),
            P("fsdp"),
            P("fsdp", None),
            P("fsdp", "tp"),
            P("fsdp", "tp"),
            P("tp", "fsdp"),
            P("fsdp", None, "tp"),
            P("fsdp", None, "tp"),
            P("fsdp", "tp", None),
        ),
        out_specs=(
            P(("fsdp", "tp"), None),
            P(("fsdp", "tp"), None),
            P("fsdp"),
            P("fsdp", "tp"),
            P("fsdp", "tp"),
            P("fsdp", "tp"),
            P("tp", "fsdp"),
            P("fsdp"),
            P("fsdp", None),
            P("fsdp", "tp"),
            P("fsdp", "tp"),
            P("tp", "fsdp"),
            P("fsdp", None, "tp"),
            P("fsdp", None, "tp"),
            P("fsdp", "tp", None),
        ),
        check_vma=False,
    )
```

```python
import jax
import jax.numpy as jnp
from jax import lax
from jax.experimental import pallas as pl
from jax.experimental.layout import Layout, with_layout_constraint
from jax.experimental.pallas import tpu as pltpu
from jax.sharding import PartitionSpec as P

QUERY_HEADS = 20
KEY_VALUE_HEADS = 4
HEAD_SIZE = 128
TOPK = 6


norm_eps = 1e-05
rope_base = 500000.0


def rotary_tables(length_total):
    half_width = HEAD_SIZE // 2
    inverse = 1.0 / rope_base ** (jnp.arange(half_width, dtype=jnp.float32) * (2.0 / HEAD_SIZE))
    angles = jnp.arange(length_total, dtype=jnp.float32)[:, None] * inverse[None, :]
    return (jnp.cos(angles), jnp.sin(angles))


def apply_rotary(values, rotary_cosine, rotary_sine):
    half_width = values.shape[-1] // 2
    first_half = values[..., :half_width]
    second_half = values[..., half_width:]
    cos_rows = rotary_cosine[:, None, :]
    sin_rows = rotary_sine[:, None, :]
    return jnp.concatenate(
        [
            first_half * cos_rows - second_half * sin_rows,
            second_half * cos_rows + first_half * sin_rows,
        ],
        axis=-1,
    )


def smooth_gate(values):
    return values / (1.0 + jnp.exp(-values))


def smooth_slope(values):
    sigmoid = 1.0 / (1.0 + jnp.exp(-values))
    return sigmoid * (1.0 + values * (1.0 - sigmoid))


def rms_scale(values):
    return lax.rsqrt(jnp.mean(values * values, axis=-1, keepdims=True) + norm_eps)


def norm_back(grad_in, normed, inv_rms, gain_vec):
    scaled = grad_in * gain_vec
    return inv_rms * (scaled - normed * jnp.mean(scaled * normed, axis=-1, keepdims=True))


def product(left_mat, right_mat):
    return jnp.dot(left_mat, right_mat, preferred_element_type=jnp.float32)


def times_transposed(left_mat, right_mat):
    return lax.dot_general(
        left_mat, right_mat, (((1,), (1,)), ((), ())), preferred_element_type=jnp.float32
    )


def transposed_times(left_mat, right_mat):
    return lax.dot_general(
        left_mat, right_mat, (((0,), (0,)), ((), ())), preferred_element_type=jnp.float32
    )


def attention_scores(query_rot, rotated_key, allowed):
    scores = jnp.einsum(
        "qgjd,kgd->gjqk", query_rot, rotated_key, preferred_element_type=jnp.float32
    ) * HEAD_SIZE ** (-0.5)
    return jnp.where(allowed, scores, -1e30)


def shards(
    tokens_in,
    cotangent,
    doc_ids,
    routes,
    gain_attn,
    w_query,
    w_key,
    w_value,
    w_out,
    gain_ffn,
    w_router,
    w_shared_gate,
    w_shared_up,
    w_shared_down,
    w_expert_gate,
    w_expert_up,
    w_expert_down,
):
    own_rows = tokens_in.shape[0]
    seq_rows = doc_ids.shape[0]
    model_width = tokens_in.shape[1]
    experts = w_router.shape[1]
    local_experts = w_expert_gate.shape[0]
    sources = experts // local_experts
    capacity = max(2, 4 * seq_rows * TOPK // (3 * experts))
    position = lax.axis_index("tp")
    gathered = (
        lax.all_gather(w_query, "fsdp", axis=0, tiled=True),
        lax.all_gather(w_key, "fsdp", axis=0, tiled=True),
        lax.all_gather(w_value, "fsdp", axis=0, tiled=True),
        lax.all_gather(w_out, "fsdp", axis=1, tiled=True),
        lax.all_gather(w_shared_gate, "fsdp", axis=0, tiled=True),
        lax.all_gather(w_shared_up, "fsdp", axis=0, tiled=True),
        lax.all_gather(w_shared_down, "fsdp", axis=1, tiled=True),
        lax.all_gather(w_router, "fsdp", axis=0, tiled=True),
        lax.all_gather(gain_attn, "fsdp", axis=0, tiled=True),
        lax.all_gather(gain_ffn, "fsdp", axis=0, tiled=True),
    )
    (
        full_query,
        full_key,
        full_value,
        full_out,
        full_sgate,
        full_sup,
        full_sdown,
        full_router,
        gain_one_low,
        gain_two_low,
    ) = gathered
    first_norm_gain = gain_one_low.astype(jnp.float32)
    second_norm_gain = gain_two_low.astype(jnp.float32)
    group_tokens, group_cot = (
        lax.all_gather(tokens_in, "tp", axis=0, tiled=True),
        lax.all_gather(cotangent, "tp", axis=0, tiled=True),
    )
    residual = group_tokens.astype(jnp.float32)
    upstream = group_cot.astype(jnp.float32)
    scale_one = rms_scale(residual)
    normed_one = residual * scale_one
    attn_input = (normed_one * first_norm_gain).astype(jnp.bfloat16)
    heads_local = full_query.shape[1] // HEAD_SIZE
    kv_local = full_key.shape[1] // HEAD_SIZE
    tokens_per_group = QUERY_HEADS // KEY_VALUE_HEADS
    rotary_cosine, rotary_sine = rotary_tables(seq_rows)
    query_rot = (
        apply_rotary(
            product(attn_input, full_query).reshape(seq_rows, heads_local, HEAD_SIZE),
            rotary_cosine,
            rotary_sine,
        )
        .astype(jnp.bfloat16)
        .reshape(seq_rows, kv_local, tokens_per_group, HEAD_SIZE)
    )
    rotated_key = apply_rotary(
        product(attn_input, full_key).reshape(seq_rows, kv_local, HEAD_SIZE),
        rotary_cosine,
        rotary_sine,
    ).astype(jnp.bfloat16)
    value_low = (
        product(attn_input, full_value).astype(jnp.bfloat16).reshape(seq_rows, kv_local, HEAD_SIZE)
    )
    order_ids = jnp.arange(seq_rows)
    allowed = (doc_ids[:, None] == doc_ids[None, :]) & (order_ids[:, None] >= order_ids[None, :])
    scores = attention_scores(query_rot, rotated_key, allowed)
    top_score = jnp.max(scores, axis=-1, keepdims=True)
    weights = jnp.exp(scores - top_score)
    weight_sum = jnp.sum(weights, axis=-1, keepdims=True)
    log_total = top_score + jnp.log(weight_sum)
    probs_low = (weights / weight_sum).astype(jnp.bfloat16)
    heads_out = (
        jnp.einsum("gjqk,kgd->qgjd", probs_low, value_low, preferred_element_type=jnp.float32)
        .astype(jnp.bfloat16)
        .reshape(seq_rows, heads_local * HEAD_SIZE)
    )
    attn_branch = lax.psum(product(heads_out, full_out), "tp")
    middle = residual + attn_branch
    scale_two = rms_scale(middle)
    normed_two = middle * scale_two
    ffn_input = (normed_two * second_norm_gain).astype(jnp.bfloat16)
    logits = product(ffn_input, full_router)
    chosen = routes[:, :, None] == jnp.arange(experts, dtype=jnp.int32)[None, None, :]
    picked = jnp.sum(jnp.where(chosen, logits[:, None, :], 0.0), axis=-1)
    top_pick = jnp.max(picked, axis=-1, keepdims=True)
    gate_exp = jnp.exp(picked - top_pick)
    gate_values = gate_exp / jnp.sum(gate_exp, axis=-1, keepdims=True)
    shared_gate = product(ffn_input, full_sgate)
    shared_up = product(ffn_input, full_sup)
    shared_act = smooth_gate(shared_gate)
    shared_hidden = (shared_act * shared_up).astype(jnp.bfloat16)
    ffn_part = product(shared_hidden, full_sdown)
    flat_routes = routes.reshape(-1)
    onehot = (flat_routes[:, None] == jnp.arange(experts, dtype=jnp.int32)[None, :]).astype(
        jnp.int32
    )
    earlier = jnp.cumsum(onehot, axis=0) - onehot
    target = flat_routes * capacity + jnp.sum(earlier * onehot, axis=1)
    source = (
        jnp.full((experts * capacity,), -1, jnp.int32)
        .at[target]
        .set(jnp.arange(seq_rows * TOPK, dtype=jnp.int32))
    )
    filled = (source >= 0)[:, None]
    safe_source = jnp.maximum(source, 0)
    zero_low = jnp.zeros((), jnp.bfloat16)
    send_rows = jnp.where(filled, ffn_input[safe_source // TOPK], zero_low).reshape(
        experts, capacity, model_width
    )
    gated_cot = (
        (gate_values[:, :, None] * upstream[:, None, :])
        .astype(jnp.bfloat16)
        .reshape(seq_rows * TOPK, model_width)
    )
    send_grads = jnp.where(filled, gated_cot[safe_source], zero_low).reshape(
        experts, capacity, model_width
    )
    arrived = lax.all_to_all(send_rows, "fsdp", split_axis=0, concat_axis=0, tiled=True)
    slot_count = arrived.shape[1]
    grouped = arrived.reshape(sources, local_experts, slot_count, model_width)
    gate_pre = jnp.einsum(
        "sjcd,jdf->sjcf", grouped, w_expert_gate, preferred_element_type=jnp.float32
    )
    up_pre = jnp.einsum("sjcd,jdf->sjcf", grouped, w_expert_up, preferred_element_type=jnp.float32)
    hidden = (smooth_gate(gate_pre) * up_pre).astype(jnp.bfloat16)
    result = jnp.einsum(
        "sjcf,jfd->sjcd", hidden, w_expert_down, preferred_element_type=jnp.float32
    ).astype(jnp.bfloat16)
    half_width = gate_pre.shape[-1]
    expert_out = result.reshape(experts, slot_count, model_width)
    gate_keep = gate_pre.reshape(experts, slot_count, half_width)
    up_keep = up_pre.reshape(experts, slot_count, half_width)
    returned = lax.all_to_all(expert_out, "fsdp", split_axis=0, concat_axis=0, tiled=True)
    picked_rows = (
        returned.reshape(experts * capacity, model_width)[target]
        .reshape(seq_rows, TOPK, model_width)
        .astype(jnp.float32)
    )
    ffn_part = ffn_part + jnp.sum(gate_values[:, :, None] * picked_rows, axis=1)
    ffn_sum = lax.psum_scatter(
        ffn_part.astype(jnp.bfloat16), "tp", scatter_dimension=0, tiled=True
    ).astype(jnp.float32)
    middle_own = lax.dynamic_slice_in_dim(middle, position * own_rows, own_rows, 0)
    block_out = (middle_own + ffn_sum).astype(jnp.bfloat16)
    gate_grad = lax.psum(jnp.sum(upstream[:, None, :] * picked_rows, axis=-1), "tp")
    arrived_grads = lax.all_to_all(send_grads, "fsdp", split_axis=0, concat_axis=0, tiled=True)
    half_width = gate_keep.shape[-1]
    grad_rows = arrived_grads.reshape(sources, local_experts, capacity, model_width)
    input_rows = arrived.reshape(sources, local_experts, capacity, model_width)
    gate_pre = gate_keep.reshape(sources, local_experts, capacity, half_width)
    up_pre = up_keep.reshape(sources, local_experts, capacity, half_width)
    expert_act = smooth_gate(gate_pre)
    expert_hidden = (expert_act * up_pre).astype(jnp.bfloat16)
    hidden_grad = jnp.einsum(
        "sjcd,jfd->sjcf", grad_rows, w_expert_down, preferred_element_type=jnp.float32
    )
    grad_expert_down = jnp.einsum(
        "sjcf,sjcd->jfd", expert_hidden, grad_rows, preferred_element_type=jnp.float32
    )
    gate_low = (hidden_grad * up_pre * smooth_slope(gate_pre)).astype(jnp.bfloat16)
    up_low = (hidden_grad * expert_act).astype(jnp.bfloat16)
    grad_expert_gate = jnp.einsum(
        "sjcd,sjcf->jdf", input_rows, gate_low, preferred_element_type=jnp.float32
    )
    grad_expert_up = jnp.einsum(
        "sjcd,sjcf->jdf", input_rows, up_low, preferred_element_type=jnp.float32
    )
    row_grads = jnp.einsum(
        "sjcf,jdf->sjcd", gate_low, w_expert_gate, preferred_element_type=jnp.float32
    ) + jnp.einsum("sjcf,jdf->sjcd", up_low, w_expert_up, preferred_element_type=jnp.float32)
    row_grads = row_grads.astype(jnp.bfloat16).reshape(experts, capacity, model_width)
    back_rows = lax.all_to_all(row_grads, "fsdp", split_axis=0, concat_axis=0, tiled=True)
    input_grad = jnp.sum(
        back_rows.reshape(experts * capacity, model_width)[target]
        .reshape(seq_rows, TOPK, model_width)
        .astype(jnp.float32),
        axis=1,
    )
    shared_hidden_grad = times_transposed(group_cot, full_sdown)
    grad_shared_down = transposed_times(shared_hidden, group_cot)
    sgate_low = (shared_hidden_grad * shared_up * smooth_slope(shared_gate)).astype(jnp.bfloat16)
    sup_low = (shared_hidden_grad * shared_act).astype(jnp.bfloat16)
    grad_shared_gate = transposed_times(ffn_input, sgate_low)
    grad_shared_up = transposed_times(ffn_input, sup_low)
    input_grad = (
        input_grad + times_transposed(sgate_low, full_sgate) + times_transposed(sup_low, full_sup)
    )
    input_grad = lax.psum(input_grad, "tp")
    pick_grad = gate_values * (gate_grad - jnp.sum(gate_values * gate_grad, axis=-1, keepdims=True))
    logit_low = jnp.sum(jnp.where(chosen, pick_grad[:, :, None], 0.0), axis=1).astype(jnp.bfloat16)
    grad_router = transposed_times(ffn_input, logit_low)
    input_grad = input_grad + times_transposed(logit_low, full_router)
    grad_gain_ffn = jnp.sum(input_grad * normed_two, axis=0)
    middle_grad = upstream + norm_back(input_grad, normed_two, scale_two, second_norm_gain)
    attn_grad_low = middle_grad.astype(jnp.bfloat16)
    grad_out = transposed_times(heads_out, attn_grad_low)
    heads_grad = (
        times_transposed(attn_grad_low, full_out)
        .astype(jnp.bfloat16)
        .reshape(seq_rows, kv_local, tokens_per_group, HEAD_SIZE)
    )
    again_scores = attention_scores(query_rot, rotated_key, allowed)
    attn_probs = jnp.exp(again_scores - log_total)
    probs_grad = jnp.einsum(
        "qgjd,kgd->gjqk", heads_grad, value_low, preferred_element_type=jnp.float32
    )
    value_grad = (
        jnp.einsum(
            "gjqk,qgjd->kgd",
            attn_probs.astype(jnp.bfloat16),
            heads_grad,
            preferred_element_type=jnp.float32,
        )
        .astype(jnp.bfloat16)
        .reshape(seq_rows, kv_local * HEAD_SIZE)
    )
    score_low = (
        attn_probs * (probs_grad - jnp.sum(attn_probs * probs_grad, axis=-1, keepdims=True))
    ).astype(jnp.bfloat16)
    query_grad = jnp.einsum(
        "gjqk,kgd->qgjd", score_low, rotated_key, preferred_element_type=jnp.float32
    ) * HEAD_SIZE ** (-0.5)
    key_grad = jnp.einsum(
        "gjqk,qgjd->kgd", score_low, query_rot, preferred_element_type=jnp.float32
    ) * HEAD_SIZE ** (-0.5)
    query_low = (
        apply_rotary(
            query_grad.reshape(seq_rows, heads_local, HEAD_SIZE), rotary_cosine, -rotary_sine
        )
        .astype(jnp.bfloat16)
        .reshape(seq_rows, heads_local * HEAD_SIZE)
    )
    key_low = (
        apply_rotary(key_grad, rotary_cosine, -rotary_sine)
        .astype(jnp.bfloat16)
        .reshape(seq_rows, kv_local * HEAD_SIZE)
    )
    grad_query = transposed_times(attn_input, query_low)
    grad_key = transposed_times(attn_input, key_low)
    grad_value = transposed_times(attn_input, value_grad)
    attn_in_grad = (
        times_transposed(query_low, full_query)
        + times_transposed(key_low, full_key)
        + times_transposed(value_grad, full_value)
    )
    attn_in_grad = lax.psum(attn_in_grad.astype(jnp.bfloat16), "tp").astype(jnp.float32)
    grad_gain_attn = jnp.sum(attn_in_grad * normed_one, axis=0)
    token_grad = middle_grad + norm_back(attn_in_grad, normed_one, scale_one, first_norm_gain)
    grad_tokens = lax.dynamic_slice_in_dim(token_grad, position * own_rows, own_rows, 0)
    everything = (
        lax.psum_scatter(grad_query, "fsdp", scatter_dimension=0, tiled=True),
        lax.psum_scatter(grad_key, "fsdp", scatter_dimension=0, tiled=True),
        lax.psum_scatter(grad_value, "fsdp", scatter_dimension=0, tiled=True),
        lax.psum_scatter(grad_out, "fsdp", scatter_dimension=1, tiled=True),
        lax.psum_scatter(grad_gain_attn, "fsdp", scatter_dimension=0, tiled=True),
        lax.psum_scatter(grad_shared_gate, "fsdp", scatter_dimension=0, tiled=True),
        lax.psum_scatter(grad_shared_up, "fsdp", scatter_dimension=0, tiled=True),
        lax.psum_scatter(grad_shared_down, "fsdp", scatter_dimension=1, tiled=True),
        lax.psum_scatter(grad_router, "fsdp", scatter_dimension=0, tiled=True),
        lax.psum_scatter(grad_gain_ffn, "fsdp", scatter_dimension=0, tiled=True),
    )
    attn_grads = everything[:5]
    ffn_grads = everything[5:]
    return (
        block_out,
        grad_tokens,
        attn_grads[4],
        attn_grads[0],
        attn_grads[1],
        attn_grads[2],
        attn_grads[3],
        ffn_grads[4],
        ffn_grads[3],
        ffn_grads[0],
        ffn_grads[1],
        ffn_grads[2],
        grad_expert_gate,
        grad_expert_up,
        grad_expert_down,
    )


PAIRS = ((4, 8), (0, 1), (9, 12), (14, 6), (15, 11), (13, 7), (5, 10), (2, 3))


class Flight:
    pass


class Take:
    def __init__(self, flight):
        self.flight = flight

    def __getattr__(self, name):
        return vars(self.flight).pop(name)


def hop(values, bit):
    count = lax.axis_size("fsdp")
    return lax.ppermute(values, "fsdp", [(i, i ^ bit) for i in range(count)])


def swap(values):
    return lax.ppermute(values, "tp", [(0, 1), (1, 0)])


def route(values, rule):
    pairs = []
    for group in range(lax.axis_size("fsdp")):
        for side in range(2):
            target = rule(group, side)
            if target is not None:
                pairs.append((group * 2 + side, target[0] * 2 + target[1]))
    return lax.ppermute(values, ("fsdp", "tp"), pairs)


def is_home(group, side):
    return (group // 4) % 2 == side


def home_far(group, side):
    return (group ^ 8, side) if is_home(group, side) else None


def home_near(group, side):
    return (group ^ 4, side) if is_home(group, side) else None


def near_home(group, side):
    return None if is_home(group, side) else (group ^ 4, side)


def home_side(group, side):
    return (group, 1 - side) if is_home(group, side) else None


def pack_out_a(group, side):
    return (group ^ 4, 1) if side == group // 8 else (group ^ 8, 0)


def pack_out_b(group, side):
    return (group, 0) if side == group // 8 else (group ^ 12, 1)


def pack_back_a(group, side):
    return (group ^ (8 if side == 0 else 4), group // 8)


def pack_back_b(group, side):
    return (group ^ (0 if side == 0 else 12), group // 8)


def plane_one(group, side):
    return (group ^ (1 if side == 0 else 2), side)


def plane_two(group, side):
    return (group ^ (2 if side == 0 else 1), side)


def cot_first_route(group, side):
    return (group ^ (8 if side == 0 else 4), side)


def cot_second_route(group, side):
    return (group ^ 4, 1) if side == 0 else None


COT_CARRIED = ((0, 8, 1, 9, 2, 10, 3, 11), (4, 12, 6, 14, 5, 13, 7, 15))
CARRIED = ((0, 8, 1, 9, 2, 10, 3, 11), (12, 4, 14, 6, 13, 5, 15, 7))


def join(*parts):
    return jnp.concatenate(parts, axis=0)


def plus(left, right):
    return (left.astype(jnp.float32) + right.astype(jnp.float32)).astype(jnp.bfloat16)


def piece(view):
    array, start, rows = view
    return array if array.shape[0] == rows else array[start : start + rows]


def whole_view(array):
    return (array, 0, array.shape[0])


def as_tuple(index):
    return index if isinstance(index, tuple) else (index,)


LINE = (0, 4, 8, 12)


def exchange_plane(block_for):
    parts = [jnp.stack([block_for(line + plane) for line in LINE]) for plane in range(4)]
    parts = [parts[0]] + [hop(parts[plane], plane) for plane in (1, 2, 3)]
    return {line: jnp.stack([part[i] for part in parts]) for i, line in enumerate(LINE)}


def exchange_line(sent, lines):
    return {line: hop(sent[line], line) if line else sent[line] for line in lines}


def exchange_join(got, me):
    rows, columns = got[0].shape[1:]
    whole = jnp.zeros((16, rows, columns), got[0].dtype)
    for line, blocks in got.items():
        for plane in range(4):
            whole = lax.dynamic_update_slice_in_dim(
                whole, blocks[plane : plane + 1], me ^ (line + plane), 0
            )
    return whole


def chosen_slots(place_ref, which, slots):
    numbers = lax.broadcasted_iota(jnp.int32, (slots, place_ref.shape[2]), 0)
    return numbers.astype(jnp.float32) == place_ref[0, which : which + 1, :]


def expert_kernel(first, number, starts, *refs):
    side_ref, tok_refs, cot_refs = refs[0], refs[1:5], refs[5:9]
    w_gate_ref, w_up_ref, w_down_ref, in_ref, out_ref = refs[9:14]
    refs = refs[14 if first else 21 :]
    stores = refs[:7]
    back_refs, note_ref = refs[7:10], refs[10]
    (
        toks,
        cots,
        rows,
        cot_rows,
        dys,
        hids,
        dboth,
        shareds,
        w_both,
        w_down,
        w_in,
        w_out,
        gate_terms,
        sems,
        store_sems,
    ) = refs[11:]
    part_rows = back_refs[0].shape[0]
    starts, spots = starts
    side = side_ref[0]
    seq_rows = 2 * part_rows
    hidden = w_down.shape[0]
    tile = 256
    slots = rows.shape[0] // 2

    parts = [pl.ds(i * part_rows, part_rows) for i in range(4)]
    pairs = [
        (tok_refs[i].at[pl.ds(starts[i], part_rows)], toks.at[parts[i]]) for i in range(4)
    ]
    pairs += [(in_ref, w_in)]
    pairs += [(None, cots.at[parts[i]]) for i in range(4)]
    pairs += [(out_ref, w_out)]
    for start in range(0, hidden, tile):
        cut = pl.ds(start, tile)
        pairs += [
            (w_gate_ref.at[0, :, cut], w_both.at[:, cut]),
            (w_up_ref.at[0, :, cut], w_both.at[:, pl.ds(hidden + start, tile)]),
            (w_down_ref.at[0, cut], w_down.at[cut]),
        ]
    def cot_copy(which, half, source):
        row = spots[which][0] * seq_rows + (side if half == 0 else 1 - side) * part_rows
        index = 5 + 2 * which + half
        return pltpu.make_async_copy(
            source.at[pl.ds(pl.multiple_of(row, part_rows), part_rows)],
            pairs[index][1],
            sems.at[index],
        )

    loads = []
    for index, (source, target) in enumerate(pairs):
        if source is None:
            which, half = divmod(index - 5, 2)
            mine, other = cot_refs[2 * which], cot_refs[2 * which + 1]
            is_mine = side == spots[which][1]

            @pl.when(is_mine)
            def start_mine(which=which, half=half, mine=mine):
                cot_copy(which, half, mine).start()

            @pl.when(jnp.logical_not(is_mine))
            def start_other(which=which, half=half, other=other):
                cot_copy(which, half, other).start()

            loads.append(cot_copy(which, half, mine))
        else:
            loads.append(pltpu.make_async_copy(source, target, sems.at[index]))
            loads[-1].start()

    sent = []

    def store(index, source):
        target = stores[index].at[pl.ds(number * source.shape[0], source.shape[0])]
        copy = pltpu.make_async_copy(source, target, store_sems.at[index])
        copy.start()
        sent.append(copy)

    gate_loads = []
    experts, term_width = gate_terms.shape[0] // 4, gate_terms.shape[1]
    for i in range(4):
        source = tok_refs[i].at[pl.ds(starts[i] + part_rows, experts), pl.ds(0, term_width)]
        target = gate_terms.at[pl.ds(i * experts, experts)]
        gate_loads.append(pltpu.make_async_copy(source, target, store_sems.at[7 + i]))
        gate_loads[-1].start()
    for load in gate_loads:
        load.wait()
    expert = side_ref[1]
    numbers = lax.broadcasted_iota(jnp.int32, (experts, term_width), 0)
    before = lax.broadcasted_iota(jnp.int32, (seq_rows, seq_rows), 0) < (
        lax.broadcasted_iota(jnp.int32, (seq_rows, seq_rows), 1)
    )
    before = before.astype(jnp.float32).astype(jnp.bfloat16)
    for which in range(2):
        halves = []
        for i in (2 * which, 2 * which + 1):
            terms = gate_terms[i * experts : (i + 1) * experts, :].astype(jnp.float32)
            row = jnp.sum(jnp.where(numbers == expert, terms, 0.0), axis=0, keepdims=True)
            halves.append(
                row[:, :part_rows]
                + row[:, part_rows : 2 * part_rows]
                + row[:, 2 * part_rows : 3 * part_rows]
            )
        gate_row = jnp.concatenate(halves, axis=1)
        flags = jnp.where(gate_row >= 0.0, 1.0, 0.0)
        ranks = product(
            jnp.broadcast_to(flags, (8, seq_rows)).astype(jnp.bfloat16), before
        )[:1]
        note_ref[2 + which : 3 + which, :] = jnp.where(flags > 0.0, ranks, -1.0)
        note_ref[4 + which : 5 + which, :] = gate_row
    for load in loads[:4]:
        load.wait()
    slot_numbers = lax.broadcasted_iota(jnp.int32, (slots, seq_rows), 0).astype(jnp.float32)
    chosen = [slot_numbers == note_ref[2 + which : 3 + which, :] for which in range(2)]
    low = [c.astype(jnp.bfloat16) for c in chosen]
    for which in range(2):
        span = slice(which * slots, (which + 1) * slots)
        seq = slice(which * seq_rows, (which + 1) * seq_rows)
        rows[span, :] = product(low[which], toks[seq, :]).astype(jnp.bfloat16)
    store(0, rows)
    store(5, toks)
    loads[4].wait()
    shared_pre = product(toks[...], w_in[...])
    for load in loads[5:9]:
        load.wait()
    gates = [
        jnp.sum(
            jnp.where(chosen[which], note_ref[4 + which : 5 + which, :], 0.0),
            axis=1,
            keepdims=True,
        )
        for which in range(2)
    ]
    for which in range(2):
        span = slice(which * slots, (which + 1) * slots)
        seq = slice(which * seq_rows, (which + 1) * seq_rows)
        picked = product(low[which], cots[seq, :])
        cot_rows[span, :] = picked.astype(jnp.bfloat16)
        dys[span, :] = (gates[which] * picked).astype(jnp.bfloat16)
    store(1, dys)
    store(6, cots)
    gates = jnp.concatenate(gates, axis=0)
    loads[9].wait()
    half = w_out.shape[0]
    pre, up = shared_pre[:, :half], shared_pre[:, half:]
    hid_grad = times_transposed(cots[...], w_out[...])
    sigmoid = 1.0 / (1.0 + jnp.exp(-pre))
    act = pre * sigmoid
    shareds[:, :half] = (hid_grad * up * (sigmoid * (1.0 + pre * (1.0 - sigmoid)))).astype(
        jnp.bfloat16
    )
    shareds[:, half : 2 * half] = (hid_grad * act).astype(jnp.bfloat16)
    shareds[:, 2 * half :] = (act * up).astype(jnp.bfloat16)
    store(4, shareds)

    picks = jnp.zeros_like(gates)
    for index, start in enumerate(range(0, hidden, tile)):
        for load in loads[10 + 3 * index : 13 + 3 * index]:
            load.wait()
        cut = slice(start, start + tile)
        cut_up = slice(hidden + start, hidden + start + tile)
        gate_pre = product(rows[...], w_both[:, cut])
        up_pre = product(rows[...], w_both[:, cut_up])
        cot_hidden = times_transposed(cot_rows[...], w_down[cut, :])
        sigmoid = 1.0 / (1.0 + jnp.exp(-gate_pre))
        act = gate_pre * sigmoid
        hid = (act * up_pre).astype(jnp.bfloat16)
        grad = gates * cot_hidden
        hids[:, cut] = hid
        dboth[:, cut] = (grad * up_pre * (sigmoid * (1.0 + gate_pre * (1.0 - sigmoid)))).astype(
            jnp.bfloat16
        )
        dboth[:, cut_up] = (grad * act).astype(jnp.bfloat16)
        picks = picks + jnp.sum(hid.astype(jnp.float32) * cot_hidden, axis=1, keepdims=True)
    store(2, hids)
    store(3, dboth)
    back_rows = times_transposed(dboth[...], w_both[...]).astype(jnp.bfloat16)
    for which in range(2):
        span = slice(which * slots, (which + 1) * slots)
        seq = slice(which * seq_rows, (which + 1) * seq_rows)
        back = transposed_times(low[which], back_rows[span, :]) + times_transposed(
            shareds[seq, : 2 * half], w_in[...]
        )
        back_refs[which][...] = back[:part_rows, :].astype(jnp.bfloat16)
        back_refs[2][which * part_rows : (which + 1) * part_rows, :] = back[
            part_rows:, :
        ].astype(jnp.bfloat16)
        note_ref[which : which + 1, :] = jnp.sum(
            jnp.where(chosen[which], picks[span, :], 0.0), axis=0, keepdims=True
        )
    for copy in sent:
        copy.wait()


def expert_call(number, position, tokens, cots, weights, kept):
    w_gate, w_up, w_down, shared_in, shared_out = weights
    experts, width = 16, tokens[0][0].shape[1]
    part_rows = tokens[0][2] - experts
    starts = (tuple(view[1] for view in tokens), tuple(cot[2:] for cot in cots))
    slots = part_rows
    hidden = w_gate.shape[2]
    calls = len(PAIRS)
    first = kept is None
    low = jnp.bfloat16
    some = pl.BlockSpec(memory_space=pl.ANY)
    backs = [pl.BlockSpec((n * part_rows, width), lambda i: (0, 0)) for n in (1, 1, 2)]
    note = pl.BlockSpec((6, 2 * part_rows), lambda i: (0, 0))
    in_specs = [pl.BlockSpec(memory_space=pltpu.SMEM)] + [some] * 13
    operands = [position, *(view[0] for view in tokens)]
    operands += [array for cot in cots for array in cot[:2]]
    operands += weights
    aliases = {}
    if not first:
        aliases = {len(operands) + i: i for i in range(7)}
        in_specs += [some] * 7
        operands += list(kept)
    shared_width = 3 * shared_out.shape[0]
    kept_shapes = [(2 * slots, width)] * 2 + [(2 * slots, hidden), (2 * slots, 2 * hidden)]
    kept_shapes += [(4 * part_rows, c) for c in (shared_width, width, width)]
    out_shape = [jax.ShapeDtypeStruct((calls * r, c), low) for r, c in kept_shapes]
    out_shape += [jax.ShapeDtypeStruct((n * part_rows, width), low) for n in (1, 1, 2)]
    out_shape += [jax.ShapeDtypeStruct((6, 2 * part_rows), jnp.float32)]
    results = pl.pallas_call(
        lambda *refs: expert_kernel(first, number, starts, *refs),
        grid=(1,),
        in_specs=in_specs,
        out_specs=[some] * 7 + backs + [note],
        out_shape=out_shape,
        scratch_shapes=[
            pltpu.VMEM((4 * part_rows, width), low),
            pltpu.VMEM((4 * part_rows, width), low),
            pltpu.VMEM((2 * slots, width), low),
            pltpu.VMEM((2 * slots, width), low),
            pltpu.VMEM((2 * slots, width), low),
            pltpu.VMEM((2 * slots, hidden), low),
            pltpu.VMEM((2 * slots, 2 * hidden), low),
            pltpu.VMEM((4 * part_rows, shared_width), low),
            pltpu.VMEM((width, 2 * hidden), low),
            pltpu.VMEM((hidden, width), low),
            pltpu.VMEM(shared_in.shape, low),
            pltpu.VMEM(shared_out.shape, low),
            pltpu.VMEM((4 * experts, 3 * part_rows), low),
            pltpu.SemaphoreType.DMA((10 + 3 * (hidden // 256),)),
            pltpu.SemaphoreType.DMA((11,)),
        ],
        input_output_aliases=aliases,
        compiler_params=pltpu.CompilerParams(vmem_limit_bytes=40 * 1024 * 1024),
        cost_estimate=pl.CostEstimate(
            flops=4 * slots * width * (5 * hidden + 10 * slots),
            bytes_accessed=24 * 1024 * 1024,
            transcendentals=slots * hidden,
        ),
        name="expert_pass",
    )(*operands)
    return results[:7], results[7:10], results[10]


def output_kernel(
    place_ref, gate_ref, hid_ref, shared_ref, w_down_ref, w_out_ref, own_ref, other_ref
):
    part_rows = own_ref.shape[0] // 2
    seq_rows = 2 * part_rows
    slots = hid_ref.shape[0] // 2
    half = w_out_ref.shape[0]
    result = product(hid_ref[...], w_down_ref[0])
    for which in range(2):
        chosen = chosen_slots(place_ref, which, slots)
        gates = jnp.sum(
            jnp.where(chosen, gate_ref[0, which : which + 1, :], 0.0), axis=1, keepdims=True
        )
        gated = (gates * result[which * slots : (which + 1) * slots, :]).astype(jnp.bfloat16)
        seq = slice(which * seq_rows, (which + 1) * seq_rows)
        out = transposed_times(chosen.astype(jnp.bfloat16), gated) + product(
            shared_ref[seq, 2 * half :], w_out_ref[...]
        )
        rows = slice(which * part_rows, (which + 1) * part_rows)
        own_ref[rows, :] = out[:part_rows, :].astype(jnp.bfloat16)
        other_ref[rows, :] = out[part_rows:, :].astype(jnp.bfloat16)


def output_call(places, gates, hids, shareds, w_down, shared_out):
    calls = len(PAIRS)
    slots, hidden = places.shape[2] // 2, hids.shape[1]
    width = shared_out.shape[1]
    tok_rows = shareds.shape[0] // calls
    row = pl.BlockSpec((1, 2, places.shape[2]), lambda i: (i, 0, 0))
    half = jax.ShapeDtypeStruct((calls * tok_rows // 2, width), jnp.bfloat16)
    return pl.pallas_call(
        output_kernel,
        grid=(calls,),
        in_specs=[
            row,
            row,
            pl.BlockSpec((2 * slots, hidden), lambda i: (i, 0)),
            pl.BlockSpec((tok_rows, shareds.shape[1]), lambda i: (i, 0)),
            pl.BlockSpec(w_down.shape, lambda i: (0, 0, 0)),
            pl.BlockSpec(shared_out.shape, lambda i: (0, 0)),
        ],
        out_specs=[pl.BlockSpec((tok_rows // 2, width), lambda i: (i, 0))] * 2,
        out_shape=[half] * 2,
        compiler_params=pltpu.CompilerParams(vmem_limit_bytes=48 * 1024 * 1024),
        cost_estimate=pl.CostEstimate(
            flops=4 * slots * width * (hidden + 4 * slots) * calls,
            bytes_accessed=32 * 1024 * 1024,
            transcendentals=0,
        ),
        name="expert_outputs",
    )(places, gates, hids, shareds, w_down, shared_out)


def gathered_shards(
    tokens_in,
    cotangent,
    doc_ids,
    routes,
    gain_attn,
    w_query,
    w_key,
    w_value,
    w_out,
    gain_ffn,
    w_router,
    w_shared_gate,
    w_shared_up,
    w_shared_down,
    w_expert_gate,
    w_expert_up,
    w_expert_down,
):
    low = jnp.bfloat16
    own_rows, width = tokens_in.shape
    seq_rows = doc_ids.shape[0]
    experts = w_router.shape[1]
    sources = lax.axis_size("fsdp")
    capacity = max(2, 4 * seq_rows * TOPK // (3 * experts))
    me = lax.axis_index("fsdp")
    side = lax.axis_index("tp")
    relative = jnp.arange(sources, dtype=jnp.int32) ^ me
    query_width, kv_width = w_query.shape[1], w_key.shape[1]
    heads_local, kv_local = query_width // HEAD_SIZE, kv_width // HEAD_SIZE
    per_kv = QUERY_HEADS // KEY_VALUE_HEADS

    state = Flight()
    take = Take(state)
    state.expert_grads = {}

    def barrier():
        vars(state).update(lax.optimization_barrier(dict(vars(state))))

    def launch(moves):
        got = []
        for name, parts in moves.items():
            for starts, ends in parts:
                starts, ends = as_tuple(starts), as_tuple(ends)
                blocks = [vars(state)[name][index] for index in starts]
                value = blocks[0] if len(blocks) == 1 else join(*blocks)
                got.append((name, ends, hop(value, starts[0] ^ ends[0])))
        return got

    def meet(got, value):
        blocks, value = lax.optimization_barrier(([block for *_, block in got], value))
        return [(*key, block) for (*key, _), block in zip(got, blocks, strict=True)], value

    def settle(got):
        for name, ends, value in got:
            rows = value.shape[0] // len(ends)
            for place, end in enumerate(ends):
                part = piece((value, place * rows, rows))
                if name not in summed:
                    vars(state)[name][end] = part
                    views[end] = (value, place * rows, rows)
                elif end in vars(state)[name]:
                    vars(state)[name][end] = plus(vars(state)[name][end], part)
                else:
                    later[name, end] = part

    def stage(moves, work=None):
        barrier()
        if work is not None:
            work()
        settle(launch(moves))

    summed = ("back", "out")
    later = {}
    views = {}

    small = jnp.concatenate([gain_attn[:, None], gain_ffn[:, None], w_router], axis=1)
    small_width = small.shape[1]
    small = jnp.pad(small, ((0, 0), (0, -small_width % 128)))
    position = jnp.stack([side, me]).astype(jnp.int32)

    layer = me // 4
    here = side == layer // 2
    home = layer % 2 == side
    parity_b = jnp.where(here, layer, layer ^ 3) % 2
    group_width = per_kv * HEAD_SIZE
    pack_width = 2 * group_width + 2 * HEAD_SIZE
    qkv_width = group_width + 2 * HEAD_SIZE
    out_t = w_out.T
    packs = [
        jnp.concatenate(
            [
                w_query[:, j * group_width : (j + 1) * group_width],
                w_key[:, j * HEAD_SIZE : (j + 1) * HEAD_SIZE],
                w_value[:, j * HEAD_SIZE : (j + 1) * HEAD_SIZE],
                out_t[:, j * group_width : (j + 1) * group_width],
                small,
            ],
            axis=1,
        )
        for j in range(kv_local)
    ]
    state.packs = tuple(
        jnp.where(parity_b == parity, packs[0], packs[1]) for parity in (1, 0)
    )
    state.tokens = tokens_in
    state.cot = cotangent

    def whole_of(own):
        other = swap(own)
        return jnp.where(side == 0, join(own, other), join(other, own))

    def carried(number, mine):
        zero, one = CARRIED[0][number], CARRIED[1][number]
        return me ^ (jnp.where(side == 0, zero, one) if mine else jnp.where(side == 0, one, zero))

    slice_width = w_shared_gate.shape[1] // sources
    pad_width = -slice_width % 128
    wide = slice_width + pad_width
    state.shared_parts = (w_shared_gate, w_shared_up, w_shared_down)

    def shard_for(index):
        return lax.dynamic_index_in_dim(shards_in, me ^ index, 0, keepdims=False)

    doc_rows = jnp.zeros((16, width), low).at[0, :seq_rows].set(doc_ids.astype(low))
    barrier()
    pack_a, pack_b = (
        route(pack, rule)
        for pack, rule in zip(take.packs, (pack_out_a, pack_out_b), strict=True)
    )
    state.base = join(pack_b, pack_a)
    state.tokens = join(whole_of(take.tokens), doc_rows)
    state.cot = whole_of(take.cot)
    barrier()
    base, whole_tokens = take.base, state.tokens
    state.early = join(base, route(base, plane_one))
    state.far = route(whole_tokens, home_far)
    state.near = route(whole_tokens, home_near)
    shared_parts = take.shared_parts
    shards_in = jnp.concatenate(
        [
            jnp.pad(
                part.reshape(part.shape[0], sources, slice_width),
                ((0, 0), (0, 0), (0, pad_width)),
            )
            for part in (*shared_parts[:2], shared_parts[2].T)
        ],
        axis=2,
    ).transpose(1, 0, 2)

    state.shards = exchange_plane(shard_for)
    barrier()
    early, far = state.early, state.far
    state.second = route(early, plane_two)
    state.early_other = swap(early)
    state.cross = route(far, home_near)
    state.shards_got = exchange_line(state.shards, (0, 12))
    barrier()
    second, early, early_other = take.second, take.early, take.early_other
    line_parts = [
        jnp.where(home, one, two)
        for one, two in ((take.tokens, take.near), (take.far, take.cross))
    ]
    token_rows = join(*(part[:seq_rows] for part in line_parts))
    docs = jnp.stack([part[seq_rows, :seq_rows] for part in line_parts])
    state.cot_one = route(state.cot, cot_first_route)
    state.shards_got.update(exchange_line(state.shards, (8,)))
    pack_rows = pack_a.shape[0]
    full_weights = jnp.zeros((width, pack_a.shape[1]), low)
    number = 0
    for part, got in ((early, early_other), (second, swap(second))):
        for place in range(part.shape[0] // pack_rows):
            rows = slice(place * pack_rows, (place + 1) * pack_rows)
            for block, mine in ((part[rows], True), (got[rows], False)):
                full_weights = lax.dynamic_update_slice_in_dim(
                    full_weights, block, carried(number, mine) * pack_rows, 0
                )
                full_weights = with_layout_constraint(
                    full_weights, Layout(major_to_minor=(0, 1))
                )
            number += 1

    rotary_cosine, rotary_sine = (
        jnp.tile(table, (2, 1)) for table in rotary_tables(seq_rows)
    )
    order_ids = jnp.arange(seq_rows)
    allowed = (docs[:, :, None] == docs[:, None, :]) & (
        order_ids[:, None] >= order_ids[None, :]
    )
    small_all = full_weights[:, pack_width:]
    gain_one = small_all[:, 0].astype(jnp.float32)
    gain_two = small_all[:, 1].astype(jnp.float32)
    full_router = small_all[:, 2:small_width]
    scale = HEAD_SIZE ** (-0.5)

    def attend():
        rows = token_rows.astype(jnp.float32)
        attn_input = (rows * rms_scale(rows) * gain_one).astype(low)
        state.attn_input = attn_input
        projected = product(attn_input, full_weights[:, :qkv_width])
        query_rot = apply_rotary(
            projected[:, :group_width].reshape(2 * seq_rows, per_kv, HEAD_SIZE),
            rotary_cosine,
            rotary_sine,
        )
        query_rot = query_rot.astype(low).reshape(2, seq_rows, per_kv, HEAD_SIZE)
        rotated_key = apply_rotary(
            projected[:, group_width : group_width + HEAD_SIZE][:, None, :],
            rotary_cosine,
            rotary_sine,
        )
        rotated_key = rotated_key.astype(low).reshape(2, seq_rows, HEAD_SIZE)
        value_low = projected[:, group_width + HEAD_SIZE :].astype(low)
        value_low = value_low.reshape(2, seq_rows, HEAD_SIZE)
        scores = (
            jnp.einsum("sqjd,skd->sjqk", query_rot, rotated_key, preferred_element_type=jnp.float32)
            * scale
        )
        scores = jnp.where(allowed[:, None], scores, -1e30)
        top_score = jnp.max(scores, axis=-1, keepdims=True)
        weights = jnp.exp(scores - top_score)
        attn_probs = weights / jnp.sum(weights, axis=-1, keepdims=True)
        probs_low = attn_probs.astype(low)
        heads_out = (
            jnp.einsum("sjqk,skd->sqjd", probs_low, value_low, preferred_element_type=jnp.float32)
            .astype(low)
            .reshape(2 * seq_rows, group_width)
        )
        state.attention = (query_rot, rotated_key, value_low, attn_probs, probs_low)
        state.heads_out = heads_out
        state.branch = times_transposed(heads_out, full_weights[:, qkv_width:pack_width]).astype(low)

    attend()
    barrier()

    own_routes = lax.dynamic_slice_in_dim(routes, side * own_rows, own_rows, 0)
    routed = jnp.any(
        own_routes[:, :, None] == jnp.arange(experts, dtype=jnp.int32)[None, None, :], axis=1
    )

    def near_sum(partial):
        own_part, far_part = partial[:seq_rows], partial[seq_rows:]
        state.far_part = plus(far_part, route(far_part, near_home))
        state.own_part = own_part.astype(jnp.float32) + route(own_part, near_home).astype(
            jnp.float32
        )

    def far_sum():
        return take.own_part + route(take.far_part, home_far).astype(jnp.float32)

    def own_of(own_sum):
        mine = lax.dynamic_slice_in_dim(own_sum, side * own_rows, own_rows, 0)
        other = lax.dynamic_slice_in_dim(own_sum, (1 - side) * own_rows, own_rows, 0)
        return jnp.where(home, mine, route(other, home_side))

    near_sum(take.branch)
    cot_whole, cot_one = take.cot, take.cot_one
    cot_two = route(cot_one, cot_second_route)
    state.cot_base = jnp.where(side == 0, join(cot_whole, cot_one), join(cot_one, cot_two))
    barrier()
    cot_base = take.cot_base
    state.cot_first = route(cot_base, plane_one)
    cot_base_other = swap(cot_base)
    state.shards_got.update(exchange_line(take.shards, (4,)))
    state.own_sum = far_sum()
    state.cot_base_other = cot_base_other
    barrier()
    own_sum, cot_base_other = take.own_sum, take.cot_base_other
    middle = tokens_in.astype(jnp.float32) + own_of(own_sum)
    state.middle = middle
    state.scale_two = scale_two = rms_scale(middle)
    normed_two = middle * scale_two
    state.normed_two = normed_two
    state.ffn = {0: (normed_two * gain_two).astype(low)}

    def cot_view(index):
        for core, order in enumerate(COT_CARRIED):
            if index in order:
                part, place = divmod(order.index(index), 2)
                if part == 3:
                    part, place = part + place, 0
                return (*cot_parts[part], place, core)

    logits = product(state.ffn[0], full_router)
    top_pick = jnp.max(jnp.where(routed, logits, -jnp.inf), axis=-1, keepdims=True)
    gate_exp = jnp.where(routed, jnp.exp(logits - top_pick), 0.0)
    gate_values = gate_exp / jnp.sum(gate_exp, axis=-1, keepdims=True)
    state.gate_values = gate_values
    rest = jnp.where(routed, gate_values, -1.0).T
    terms = []
    for _ in range(3):
        terms.append(rest.astype(low))
        rest = rest - terms[-1].astype(jnp.float32)
    gate_rows = jnp.concatenate(terms, axis=1)
    gate_rows = jnp.pad(gate_rows, ((0, 0), (0, width - gate_rows.shape[1])))
    ffn_own = state.ffn[0]
    state.ffn[0] = join(ffn_own, gate_rows)
    block_rows = own_rows + experts

    views[0] = whole_view(state.ffn[0])
    other_views = {}
    swapping = []

    def swap_tokens(indices):
        blocks = [state.ffn[index] for index in indices]
        others = swap(blocks[0] if len(blocks) == 1 else join(*blocks))
        for place, index in enumerate(indices):
            swapping.append((index, (others, place * block_rows, block_rows)))

    def swapped():
        other_views.update(dict(swapping))
        swapping.clear()

    barrier()
    cot_first = take.cot_first
    cot_parts = {0: (cot_base, cot_base_other)}
    cot_third = route(cot_base, plane_two)
    state.cot_third = cot_third
    got = launch(dict(ffn=((0, 8), (0, 4), (0, 1), (0, 2))))
    settle(got)
    swapped()
    shared_all = exchange_join(take.shards_got, me).reshape(width, 3 * wide)
    state.shared_in = shared_all[:, : 2 * wide]
    state.shared_out = shared_all[:, 2 * wide :].T

    state.back, state.back_own, state.back_other, state.notes = {}, {}, {}, {}
    kept = None

    def experts_of(*numbers):
        def work():
            nonlocal kept
            for number in numbers:
                one, two = PAIRS[number]
                kept, back, state.notes[number] = expert_call(
                    number,
                    position,
                    (views[one], other_views[one], views[two], other_views[two]),
                    (cot_view(one), cot_view(two)),
                    (
                        w_expert_gate,
                        w_expert_up,
                        w_expert_down,
                        state.shared_in,
                        state.shared_out,
                    ),
                    kept,
                )
                state.back_own[one], state.back_own[two] = back[:2]
                state.back_other[one, two] = back[2]

        return work

    def swap_back():
        ((indices, both_rows),) = state.back_other.items()
        state.back_other.clear()
        others = swap(both_rows)
        return [
            (index, others[place * own_rows : (place + 1) * own_rows])
            for place, index in enumerate(indices)
        ]

    def merge_back(fresh):
        for index, other in fresh:
            total = plus(state.back_own.pop(index), other)
            if ("back", index) in later:
                total = plus(total, later.pop(("back", index)))
            state.back[index] = total

    def both(*works):
        def work():
            for one in works:
                one()

        return work

    plan = (
        ((4, 8, 0, 1), dict(ffn=((8, 12), (8, 9), (8, 10)))),
        ((9, 12, 2), dict(ffn=((12, 14), (2, 6), (12, 13)))),
        ((14, 6, 10), dict(ffn=((13, 15), (1, 5), (10, 11)))),
        ((13, 15, 11), dict(ffn=((2, 3), (5, 7)))),
        ((5, 3, 7), dict(back=((9, 8),))),
        ((), dict(back=((14, 12), (6, 2)))),
        ((), dict(back=((15, 13), (11, 10)))),
        ((), dict(back=((13, 12), (7, 3)))),
    )
    fresh = []
    state.cot_lasts = {}
    for number, (arrived, moves) in enumerate(plan):
        barrier()
        if state.back_other:
            fresh = swap_back()
        if arrived:
            swap_tokens(arrived)
        if number == 0:
            swapped()
            cot_parts[1] = (cot_first, swap(cot_first))
        if number == 4:
            cot_third = take.cot_third
            cot_parts[2] = (cot_third, swap(cot_third))
        if number in (0, 1):
            state.cot_lasts[number] = route(
                cot_first[number * seq_rows : (number + 1) * seq_rows], plane_two
            )
        if number in (2, 3):
            cot_last = state.cot_lasts.pop(3 - number)
            cot_parts[6 - number] = (cot_last, swap(cot_last))
        experts_of(number)()
        got, state.notes[number] = meet(launch(moves), state.notes[number])
        settle(got)
        swapped()
        merge_back(fresh)
        fresh = []
    barrier()
    fresh = swap_back()
    merge_back(fresh)
    del state.ffn
    state.kept = kept

    def outputs():
        hids, shareds = state.kept[2], state.kept[4]
        notes = jnp.stack([state.notes[number] for number in range(len(PAIRS))])
        state.out_own, state.out_other = output_call(
            notes[:, 2:4],
            notes[:, 4:],
            hids,
            shareds,
            w_expert_down,
            state.shared_out,
        )

    def return_picks():
        picks = jnp.concatenate([state.notes[number][:2] for number in range(len(PAIRS))], axis=0)
        picks = picks[:, :own_rows] + swap(picks[:, own_rows:])
        picks = picks[jnp.argsort(jnp.asarray(PAIRS).reshape(-1))]
        state.gate_grad = lax.all_to_all(
            picks[relative], "fsdp", split_axis=0, concat_axis=0, tiled=True
        ).T

    def expert_grads(which):
        def work():
            slot_rows, slot_dy, hids, dboth = state.kept[:4]
            hidden = hids.shape[1]
            left, right = (
                (hids, slot_dy),
                (slot_rows, dboth[:, :hidden]),
                (slot_rows, dboth[:, hidden:]),
            )[which]
            state.expert_grads[which] = transposed_times(left, right)[None]

        return work

    def shared_grads():
        shareds, all_rows, all_cots = state.kept[4:]
        both_grads = jnp.concatenate(
            [
                transposed_times(all_rows, shareds[:, : 2 * wide]),
                transposed_times(all_cots, shareds[:, 2 * wide :]),
            ],
            axis=1,
        )
        state.shared_grads = both_grads.astype(low).reshape(
            sources, width // sources, 3 * wide
        )

    def shared_grad_for(index):
        return lax.dynamic_index_in_dim(state.shared_grads, me ^ index, 0, keepdims=False)

    outputs()
    got, state.out_own = meet(
        launch(dict(back=((10, 8), ((5, 12), (1, 8))))), state.out_own
    )
    settle(got)
    barrier()
    return_picks()
    shared_grads()
    got, state.shared_grads = meet(
        launch(dict(back=((8, 0), ((3, 1), (2, 0))))), state.shared_grads
    )
    settle(got)
    out_own_rows, out_other_rows = take.out_own, swap(take.out_other)
    state.out_other_rows = out_other_rows
    barrier()
    settle(launch(dict(back=((4, 0), (2, 0)))))
    state.shards = exchange_plane(shared_grad_for)
    out_other_rows = take.out_other_rows
    state.out = {}
    for number, index in enumerate(index for pair in PAIRS for index in pair):
        rows = slice(number * own_rows, (number + 1) * own_rows)
        state.out[index] = plus(out_own_rows[rows], out_other_rows[rows])
    def middle_back():
        gate_values, gate_grad = state.gate_values, state.gate_grad
        normed_two, ffn_input = state.normed_two, ffn_own
        pick_grad = gate_values * (
            gate_grad - jnp.sum(gate_values * gate_grad, axis=-1, keepdims=True)
        )
        logit_low = jnp.where(routed, pick_grad, 0.0).astype(low)
        input_grad = state.back.pop(0).astype(jnp.float32)
        grad_router = transposed_times(ffn_input, logit_low)
        input_grad = input_grad + times_transposed(logit_low, full_router)
        grad_gain_ffn = jnp.sum(input_grad * normed_two, axis=0)
        middle_grad = cotangent.astype(jnp.float32) + norm_back(
            input_grad, normed_two, state.scale_two, gain_two
        )
        state.middle_grad = middle_grad
        state.small_two = jnp.concatenate([grad_gain_ffn[:, None], grad_router], axis=1)
        state.attn_grad = middle_grad.astype(low)

    def attention_back():
        attn_grad_low = take.attn_grad
        full_qkv, full_out = full_weights[:, :qkv_width], full_weights[:, qkv_width:pack_width]
        query_rot, rotated_key, value_low, attn_probs, probs_low = state.attention
        heads_grad = (
            product(attn_grad_low, full_out).astype(low).reshape(2, seq_rows, per_kv, HEAD_SIZE)
        )
        probs_grad = jnp.einsum(
            "sqjd,skd->sjqk", heads_grad, value_low, preferred_element_type=jnp.float32
        )
        value_grad = (
            jnp.einsum("sjqk,sqjd->skd", probs_low, heads_grad, preferred_element_type=jnp.float32)
            .astype(low)
            .reshape(2 * seq_rows, HEAD_SIZE)
        )
        score_low = (
            attn_probs * (probs_grad - jnp.sum(attn_probs * probs_grad, axis=-1, keepdims=True))
        ).astype(low)
        query_grad = (
            jnp.einsum("sjqk,skd->sqjd", score_low, rotated_key, preferred_element_type=jnp.float32)
            * scale
        )
        key_grad = (
            jnp.einsum("sjqk,sqjd->skd", score_low, query_rot, preferred_element_type=jnp.float32)
            * scale
        )
        query_low = apply_rotary(
            query_grad.reshape(2 * seq_rows, per_kv, HEAD_SIZE), rotary_cosine, -rotary_sine
        )
        key_low = apply_rotary(
            key_grad.reshape(2 * seq_rows, 1, HEAD_SIZE), rotary_cosine, -rotary_sine
        )
        qkv_low = jnp.concatenate(
            [
                query_low.astype(low).reshape(2 * seq_rows, group_width),
                key_low.astype(low).reshape(2 * seq_rows, HEAD_SIZE),
                value_grad,
            ],
            axis=1,
        )
        attn_in_grad = times_transposed(qkv_low, full_qkv)
        state.attn_in_grad = attn_in_grad.astype(low)
        rows = token_rows.astype(jnp.float32)
        grad_gain_attn = jnp.sum(attn_in_grad * (rows * rms_scale(rows)), axis=0)
        small_grads = jnp.concatenate([grad_gain_attn[:, None], take.small_two], axis=1)
        grads = jnp.concatenate(
            [
                transposed_times(state.attn_input, qkv_low).astype(low),
                transposed_times(attn_grad_low, state.heads_out).astype(low),
                jnp.pad(small_grads.astype(low), ((0, 0), (0, -small_width % 128))),
            ],
            axis=1,
        )
        state.grads = with_layout_constraint(grads, Layout(major_to_minor=(0, 1)))

    def split_grads():
        grads = take.grads
        return tuple(
            join(
                *(
                    lax.dynamic_slice_in_dim(grads, carried(n, mine) * pack_rows, pack_rows, 0)
                    for n in range(len(CARRIED[0]))
                )
            )
            for mine in (True, False)
        )

    barrier()
    middle_back()
    state.whole = whole_of(take.attn_grad)
    barrier()
    whole_grad = state.whole
    state.far = route(whole_grad, home_far)
    state.near = route(whole_grad, home_near)
    expert_grads(0)()
    got, state.expert_grads[0] = meet(
        launch(dict(out=(((3, 1), (2, 0)), ((15, 14), (13, 12))))), state.expert_grads[0]
    )
    settle(got)
    barrier()
    state.cross = route(state.far, home_near)
    expert_grads(1)()
    got, state.expert_grads[1] = meet(
        launch(dict(out=(((11, 13), (10, 12)), ((7, 2), (5, 0))))), state.expert_grads[1]
    )
    settle(got)
    state.shards_got = exchange_line(state.shards, (0, 4, 12))
    barrier()
    state.attn_grad = jnp.where(
        home,
        join(take.whole, take.far),
        join(take.near, take.cross),
    )
    attention_back()
    barrier()
    kept_part, sent_part = split_grads()
    state.total = plus(kept_part, swap(sent_part))
    near_sum(take.attn_in_grad)
    state.shards_got.update(exchange_line(take.shards, (8,)))
    settle(launch(dict(out=(((9, 5), (8, 4)), ((10, 6), (8, 4))))))
    expert_grads(2)()
    barrier()
    rows = state.total.shape[0] // 2
    state.total = plus(state.total[:rows], route(state.total[rows:], plane_two))
    state.own_sum = far_sum()
    settle(launch(dict(out=((12, 8),))))
    barrier()
    settle(launch(dict(out=((8, 0), (4, 0)))))
    shared_back = exchange_join(take.shards_got, me)
    shared_back = shared_back.transpose(1, 0, 2).astype(jnp.float32)
    state.shared_sums = [
        shared_back[:, :, i * wide : i * wide + slice_width].reshape(width // sources, -1)
        for i in range(3)
    ]
    rows = state.total.shape[0] // 2
    state.total = plus(state.total[:rows], route(state.total[rows:], plane_one))
    attn_in_grad = own_of(take.own_sum)
    tokens_float = tokens_in.astype(jnp.float32)
    scale_one = rms_scale(tokens_float)
    normed_own = tokens_float * scale_one
    state.grad_tokens = take.middle_grad + norm_back(
        attn_in_grad, normed_own, scale_one, gain_one
    )
    barrier()
    part_b = route(state.total[:pack_rows], pack_back_b).astype(jnp.float32)
    part_a = route(state.total[pack_rows:], pack_back_a).astype(jnp.float32)
    packs_back = (
        jnp.where(parity_b == 0, part_b, part_a),
        jnp.where(parity_b == 0, part_a, part_b),
    )

    grad_shared_gate, grad_shared_up, grad_shared_down = state.shared_sums
    small_sum = sum(part[:, pack_width : pack_width + small_width] for part in packs_back)
    small_sum = small_sum + swap(small_sum)
    block_out = (state.middle + state.out[0].astype(jnp.float32)).astype(low)
    cuts = (0, group_width, group_width + HEAD_SIZE, qkv_width, pack_width)
    grad_query, grad_key, grad_value, grad_out_t = (
        jnp.concatenate([part[:, start:stop] for part in packs_back], axis=1)
        for start, stop in zip(cuts[:-1], cuts[1:], strict=True)
    )
    return (
        block_out,
        state.grad_tokens,
        small_sum[:, 0],
        grad_query,
        grad_key,
        grad_value,
        grad_out_t.T,
        small_sum[:, 1],
        small_sum[:, 2:],
        grad_shared_gate,
        grad_shared_up,
        grad_shared_down.T,
        state.expert_grads[1],
        state.expert_grads[2],
        state.expert_grads[0],
    )


def solution(mesh):
    wide = mesh.shape["fsdp"] == 16 and mesh.shape["tp"] == 2
    return jax.shard_map(
        gathered_shards if wide else shards,
        mesh=mesh,
        in_specs=(
            P(("fsdp", "tp"), None),
            P(("fsdp", "tp"), None),
            P("fsdp"),
            P("fsdp", None),
            P("fsdp"),
            P("fsdp", "tp"),
            P("fsdp", "tp"),
            P("fsdp", "tp"),
            P("tp", "fsdp"),
            P("fsdp"),
            P("fsdp", None),
            P("fsdp", "tp"),
            P("fsdp", "tp"),
            P("tp", "fsdp"),
            P("fsdp", None, "tp"),
            P("fsdp", None, "tp"),
            P("fsdp", "tp", None),
        ),
        out_specs=(
            P(("fsdp", "tp"), None),
            P(("fsdp", "tp"), None),
            P("fsdp"),
            P("fsdp", "tp"),
            P("fsdp", "tp"),
            P("fsdp", "tp"),
            P("tp", "fsdp"),
            P("fsdp"),
            P("fsdp", None),
            P("fsdp", "tp"),
            P("fsdp", "tp"),
            P("tp", "fsdp"),
            P("fsdp", None, "tp"),
            P("fsdp", None, "tp"),
            P("fsdp", "tp", None),
        ),
        check_vma=False,
    )
```
